128 devices in a mesh: ctx: 32 (over z, y, x_hi), exp: 4 (over x_lo, core).
Axes of the slice: x: 4 (x_hi: 2, x_lo: 2; x = x_hi * 2 + x_lo), y: 4, z: 4, core: 2. Of those that a mesh axis runs over, the one named last changes fastest.
Arguments:
- residual_in: bfloat16 [4096, 3072], P('ctx', 'exp'), may hold values from -6 to 6
- residual_tan: bfloat16 [4096, 3072], P('ctx', 'exp'), may hold values from -6 to 6
- queries: bfloat16 [4096, 1536], P('ctx', 'exp'), may hold values from -96 to 96
- keys: bfloat16 [4096, 1536], P('ctx', 'exp'), may hold values from -4 to 4
- values: bfloat16 [4096, 1536], P('ctx', 'exp'), may hold values from -6 to 6
- query_tan: bfloat16 [4096, 1536], P('ctx', 'exp'), may hold values from -6 to 6
- key_tan: bfloat16 [4096, 1536], P('ctx', 'exp'), may hold values from -6 to 6
- value_tan: bfloat16 [4096, 1536], P('ctx', 'exp'), may hold values from -6 to 6
- out_proj: bfloat16 [1536, 3072], P('exp'), may hold values from -0.15625 to 0.15625
- shift_mod: float32 [3072], replicated, may hold values from -3 to 3
- scale_mod: float32 [3072], replicated, may hold values from -1.5 to 1.5
- router: bfloat16 [3072, 16], replicated, may hold values from -0.109375 to 0.109375
- up_weight: bfloat16 [32, 3072, 6144], P('ctx', None, 'exp'), may hold values from -0.109375 to 0.109375
- down_weight: bfloat16 [32, 6144, 3072], P('ctx', 'exp'), may hold values from -0.0546875 to 0.0546875
- expert_ids: int32 [4096, 2], P('ctx'), may hold values from 0 to 15, all different within a row; in each aligned block of 128 rows (0 to 127, 128 to 255, ...) at most 20 rows name the same one
Outputs:
- mixed: bfloat16 [4096, 3072], P('ctx', 'exp')
- mixed_tan: bfloat16 [4096, 3072], P('ctx', 'exp')
The draws below stay inside these ranges and needn't reach their ends.
Inputs may be any that keep to these rules, and one draw needn't show every extreme that they name: `expert_ids`: each row names two different experts. Among the 128 rows of one ctx index no expert is named more than 20 times, and in some such block one expert is named exactly 20 times; every expert is named by some row.
All inputs are finite; a program needn't handle non-finite values.
Results may differ from the reference program's by a relative error of at most 0.018.
Values may be sent and summed in bfloat16 or wider, within the bound.
A program may use at most 192 MiB of HBM per device.

```python
import math
import jax
import jax.numpy as jnp
import numpy as np
from jax import lax

D = 3072
HEADS = 12
HD = 128
FF = 12288
EXPERTS = 16
TOK = 128
TOKENS = 4096
SPLIT = 2
CAP = 20
N_CTX = 32
N_EXP = 4


def shared_keys(key):
    width = HEADS * HD
    base = jnp.clip(jax.random.normal(jax.random.fold_in(key, 6), (TOKENS, width), jnp.float32), -3.5, 3.5)
    chosen = jax.random.randint(jax.random.fold_in(key, 5), (8,), 0, TOKENS - 1)
    mixed_rows = base[chosen + 1]
    base = base.at[chosen + 1].set(mixed_rows)
    return base


def align_rows(key, plain, key_rows, strength):
    blocks = TOKENS // TOK
    index = jnp.arange(blocks, dtype=jnp.int32)
    first = jax.random.randint(jax.random.fold_in(key, 11), (blocks,), 0, TOK)
    gap = jax.random.randint(jax.random.fold_in(key, 12), (blocks,), 0, TOK - 1)
    second = (first + 1 + gap) % TOK
    sources = jax.random.randint(jax.random.fold_in(key, 13), (2, blocks), 0, TOK)
    before = (index - 1) % blocks * TOK + sources[0]
    across = (index + blocks // 2) % blocks * TOK + sources[1]
    plain = plain.at[index * TOK + first].set(strength * key_rows[before])
    return plain.at[index * TOK + second].set(strength * key_rows[across])


def draw_keys(key, part):
    result = shared_keys(key)
    return result.astype(jnp.bfloat16)


def draw_queries(key, part):
    base = shared_keys(key)
    key = jax.random.fold_in(key, 3)
    plain = jnp.clip(jax.random.normal(key, (TOKENS, HEADS * HD), jnp.float32), -4.0, 4.0)
    return align_rows(key, plain, base, 2.0).astype(jnp.bfloat16)


def steps_of(stream_key, dims, shards, low, top_value):
    factor_of, own = 1.0, jax.random.fold_in(stream_key, 6)
    for dim, parts in shards:
        draws = jnp.exp(jax.random.uniform(jax.random.fold_in(own, dim), (parts,), jnp.float32, low / len(shards), top_value / len(shards)))
        factor_of = factor_of * jnp.repeat(draws, dims[dim] // parts).reshape([-1 if axis == dim else 1 for axis in range(len(dims))])
    return factor_of


def shared_out(own_key, own, number, rows, number_of, top, bound, lean):
    order = jax.random.permutation(own_key, number_of)
    crowded, common = shares(number_of, rows * top, bound, lean, True), shares(number_of, rows * top, bound, lean, False)
    places = jnp.arange(number_of)

    def named(sizes, offset_by):
        used = int((sizes > 0).sum())
        fixed = max(1, used // 4)
        passed = fixed + (places - fixed + offset_by * (used - fixed)) % max(1, number_of - fixed)
        return jnp.zeros((number_of,), jnp.int32).at[order[jnp.where(places < fixed, places, passed)]].set(jnp.asarray(sizes, jnp.int32))

    sizes = jnp.where(number % 4 == 0, named(crowded, number // 4), named(common, number - number // 4 - 1))
    mixed = jax.random.permutation(jax.random.fold_in(own, 3), number_of)
    source_of, taker = mixed[0:number_of // 2 * 2:2], mixed[1:number_of // 2 * 2:2]
    slack = jnp.minimum(sizes[source_of] - 1, bound - sizes[taker]) // 2
    slack = jnp.where((source_of == order[0]) | (taker == order[0]) | (sizes[taker] == 0), 0, jnp.maximum(slack, 0))
    passed = jax.random.randint(jax.random.fold_in(own, 4), (number_of // 2,), 0, 1 << 20) % (slack + 1)
    sizes = sizes.at[source_of].add(-passed).at[taker].add(passed)
    items = jnp.searchsorted(jnp.cumsum(sizes), jnp.arange(rows * top), side="right").astype(jnp.int32)
    table = items.reshape(top, rows).T
    table = table[jax.random.permutation(jax.random.fold_in(own, 1), rows)]
    offset_by = jax.random.randint(jax.random.fold_in(own, 2), (rows, 1), 0, top)
    return jnp.take_along_axis(table, (jnp.arange(top)[None, :] + offset_by) % top, axis=1)


def shares(number_of, total, bound, skew, full):
    loads = [(1 << 20) // math.isqrt(standing ** skew) + 1 for standing in range(1, number_of + 1)]
    largest = bound if full else min(bound, max(-(-total // number_of), total * loads[0] // sum(loads)))
    least = 1 if total - largest >= number_of - 1 else 0
    holding, rest = [largest] + [least] * (number_of - 1), total - largest - least * (number_of - 1)
    while rest > 0:
        free = [i for i in range(1, number_of) if holding[i] < largest] or [i for i in range(1, number_of) if holding[i] < bound]
        whole, left = sum([loads[i] for i in free]), rest
        for i in free:
            more = min(bound - holding[i], max(1, left * loads[i] // whole), rest)
            holding[i] = holding[i] + more
            rest = rest - more
    return np.array(holding)


def noise(stream_key, shape, scale, reach, shards=(), kind=jnp.bfloat16):
    values = jax.random.normal(stream_key, shape, jnp.float32) * scale
    if len(shards) > 0:
        values = steps_of(stream_key, shape, shards, -0.22, 0.18) * values
    return jnp.clip(values, min=-reach, max=reach).astype(kind)


def setup_inputs(seed: int = 0) -> dict:
    splits = jax.random.split(jax.random.key(seed), 16)
    residual_in = noise(splits[0], (TOKENS, D), 1.0, 6.0, ((0, 32), (1, 4)))
    residual_tan = noise(splits[1], (TOKENS, D), 1.0, 6.0, ((0, 32), (1, 4)))
    queries = draw_queries(jax.random.fold_in(splits[15], 71), 0)
    keys = draw_keys(jax.random.fold_in(splits[15], 71), 0)
    values = noise(splits[4], (TOKENS, HEADS * HD), 1.0, 6.0, ((0, 32), (1, 4)))
    query_tan = noise(splits[5], (TOKENS, HEADS * HD), 1.0, 6.0, ((0, 32), (1, 4)))
    key_tan = noise(splits[6], (TOKENS, HEADS * HD), 1.0, 6.0, ((0, 32), (1, 4)))
    value_tan = noise(splits[7], (TOKENS, HEADS * HD), 1.0, 6.0, ((0, 32), (1, 4)))
    out_proj = noise(splits[8], (HEADS * HD, D), (HEADS * HD) ** -0.5, 0.15625, ((0, 4),))
    shift_mod = noise(splits[9], (D,), 0.5, 3.0, (), jnp.float32)
    scale_mod = noise(splits[10], (D,), 0.3, 1.5, (), jnp.float32)
    router = noise(splits[11], (D, EXPERTS), D ** -0.5, 0.109375)
    up_weight = noise(splits[12], (EXPERTS * SPLIT, D, FF // SPLIT), D ** -0.5, 0.109375, ((0, 32), (2, 4)))
    down_weight = noise(splits[13], (EXPERTS * SPLIT, FF // SPLIT, D), FF ** -0.5, 0.0546875, ((0, 32), (1, 4)))
    expert_ids_keys = jax.random.split(jax.random.fold_in(splits[14], 1), TOKENS // TOK)
    expert_ids_turns = jax.random.permutation(jax.random.fold_in(splits[14], 3), TOKENS // TOK)
    expert_ids = jax.vmap(lambda own, number: shared_out(jax.random.fold_in(splits[14], 2), own, number, TOK, EXPERTS, 2, CAP, 2))(expert_ids_keys, expert_ids_turns).reshape((TOKENS, 2))
    return {"residual_in": residual_in, "residual_tan": residual_tan, "queries": queries, "keys": keys, "values": values, "query_tan": query_tan, "key_tan": key_tan, "value_tan": value_tan, "out_proj": out_proj, "shift_mod": shift_mod, "scale_mod": scale_mod, "router": router, "up_weight": up_weight, "down_weight": down_weight, "expert_ids": expert_ids}


EPS = 1e-06

def gelu_tanh(inputs):
    return jax.nn.gelu(inputs, approximate=True)

def modulate(state_f, tan_f, meansq, cross, shift_part, scale_part):
    recip = lax.rsqrt(meansq + EPS)
    unit = state_f * recip
    unit_tan = tan_f * recip - state_f * (recip * recip * recip) * cross
    normed = (unit * (1.0 + scale_part) + shift_part).astype(jnp.bfloat16)
    normed_tan = (unit_tan * (1.0 + scale_part)).astype(jnp.bfloat16)
    return (normed, normed_tan)

def gating(logits, logit_tan, expert_ids):
    picker = (expert_ids[:, :, None] == jnp.arange(logits.shape[1], dtype=jnp.int32)[None, None, :]).astype(jnp.float32)
    own = lax.optimization_barrier(jnp.sum(picker * logits[:, None, :], axis=2))
    own_tan = lax.optimization_barrier(jnp.sum(picker * logit_tan[:, None, :], axis=2))
    other = own[:, ::-1]
    other_tan = own_tan[:, ::-1]
    gates = 1.0 / (1.0 + jnp.exp(other - own))
    gates_tan = gates * (1.0 - gates) * (own_tan - other_tan)
    return (gates, gates_tan)

def slot_targets(block_ids, experts, capacity):
    flat_ids = block_ids.reshape(-1)
    onehot = (flat_ids[:, None] == jnp.arange(experts, dtype=jnp.int32)[None, :]).astype(jnp.int32)
    ranks = jnp.cumsum(onehot, axis=0) - onehot
    within = lax.optimization_barrier(jnp.sum(ranks * onehot, axis=1))
    return flat_ids * capacity + within

def attend_head(operands):
    query, key_h, value_h, query_t, key_t, value_t = operands
    factor = HD ** (-0.5)
    scores = jnp.dot(query, key_h.T, preferred_element_type=jnp.float32) * factor
    score_tan = (jnp.dot(query_t, key_h.T, preferred_element_type=jnp.float32) + jnp.dot(query, key_t.T, preferred_element_type=jnp.float32)) * factor
    highest = lax.optimization_barrier(jnp.max(scores, axis=1, keepdims=True))
    weights = jnp.exp(scores - highest)
    denominator = lax.optimization_barrier(jnp.sum(weights, axis=1))
    mass = lax.optimization_barrier(jnp.sum(weights * score_tan, axis=1))
    weights_b = weights.astype(jnp.bfloat16)
    tilted_b = (weights * score_tan).astype(jnp.bfloat16)
    accum = jnp.dot(weights_b, value_h, preferred_element_type=jnp.float32)
    taccum = jnp.dot(tilted_b, value_h, preferred_element_type=jnp.float32) + jnp.dot(weights_b, value_t, preferred_element_type=jnp.float32)
    head_out = accum / denominator[:, None]
    head_tan = taccum / denominator[:, None] - head_out * (mass / denominator)[:, None]
    return (head_out, head_tan)

def split_heads(matrix):
    return matrix.reshape(TOKENS, HEADS, HD).transpose(1, 0, 2)

def reference(residual_in, residual_tan, queries, keys, values, query_tan, key_tan, value_tan, out_proj, shift_mod, scale_mod, router, up_weight, down_weight, expert_ids):
    operands = tuple((split_heads(item) for item in (queries, keys, values, query_tan, key_tan, value_tan)))
    head_out, head_tan = lax.map(attend_head, operands)
    attended = head_out.transpose(1, 0, 2).reshape(TOKENS, HEADS * HD).astype(jnp.bfloat16)
    attended_tan = head_tan.transpose(1, 0, 2).reshape(TOKENS, HEADS * HD).astype(jnp.bfloat16)
    state = (residual_in.astype(jnp.float32) + jnp.dot(attended, out_proj, preferred_element_type=jnp.float32)).astype(jnp.bfloat16)
    state_tan = (residual_tan.astype(jnp.float32) + jnp.dot(attended_tan, out_proj, preferred_element_type=jnp.float32)).astype(jnp.bfloat16)
    state_f = state.astype(jnp.float32)
    stan_f = state_tan.astype(jnp.float32)
    meansq = lax.optimization_barrier(jnp.mean(state_f * state_f, axis=1, keepdims=True))
    cross = lax.optimization_barrier(jnp.mean(state_f * stan_f, axis=1, keepdims=True))
    normed, normed_tan = modulate(state_f, stan_f, meansq, cross, shift_mod, scale_mod)
    logits = jnp.dot(normed, router, preferred_element_type=jnp.float32)
    logit_tan = jnp.dot(normed_tan, router, preferred_element_type=jnp.float32)
    gates, gates_tan = gating(logits, logit_tan, expert_ids)
    block_ids = expert_ids.reshape(N_CTX, TOK, 2)
    targets = jax.vmap(lambda item: slot_targets(item, EXPERTS, CAP))(block_ids)
    flat_block_ids = block_ids.reshape(N_CTX, 2 * TOK)
    within = targets - flat_block_ids * CAP
    anchor = jnp.arange(N_CTX, dtype=jnp.int32)[:, None] * CAP
    places = (flat_block_ids * (N_CTX * CAP) + anchor + within).reshape(-1).astype(jnp.int32)
    slots_all = EXPERTS * N_CTX * CAP
    owner = jnp.arange(TOKENS * 2, dtype=jnp.int32) // 2
    token_of = jnp.zeros((slots_all,), jnp.int32).at[places].set(owner).reshape(EXPERTS, N_CTX * CAP)
    live = jnp.zeros((slots_all,), jnp.float32).at[places].set(1.0).reshape(EXPERTS, N_CTX * CAP)
    gate_of = jnp.zeros((slots_all,), jnp.float32).at[places].set(gates.reshape(-1)).reshape(EXPERTS, N_CTX * CAP)
    gtan_of = jnp.zeros((slots_all,), jnp.float32).at[places].set(gates_tan.reshape(-1)).reshape(EXPERTS, N_CTX * CAP)
    blocks = SPLIT * N_EXP
    block_size = FF // blocks
    up_pieces = up_weight.reshape(EXPERTS, SPLIT, D, FF // SPLIT)
    down_whole = down_weight.reshape(EXPERTS, FF, D)

    def expert_step(carry, item):
        moe, moe_tan = carry
        tokens_here, live_here, gate_here, gtan_here, w_pieces, w_out = item
        w_in = w_pieces.transpose(1, 0, 2).reshape(D, FF)
        rows = normed[tokens_here]
        rows_tan = normed_tan[tokens_here]
        pre = jnp.dot(rows, w_in, preferred_element_type=jnp.float32)
        pre_tan = jnp.dot(rows_tan, w_in, preferred_element_type=jnp.float32)
        act, act_tan = jax.jvp(gelu_tanh, (pre,), (pre_tan,))
        act_q = act.astype(jnp.bfloat16).astype(jnp.float32).reshape(-1, blocks, block_size)
        act_tan_q = act_tan.astype(jnp.bfloat16).astype(jnp.float32).reshape(-1, blocks, block_size)
        w_out_q = w_out.astype(jnp.float32).reshape(blocks, block_size, D)
        partial_value = jnp.einsum('rqf,qfd->qrd', act_q, w_out_q, precision=lax.Precision.HIGHEST)
        partial_tan = jnp.einsum('rqf,qfd->qrd', act_tan_q, w_out_q, precision=lax.Precision.HIGHEST)
        piece = lax.optimization_barrier(jnp.sum(partial_value.astype(jnp.bfloat16).astype(jnp.float32), axis=0))
        piece_tan = lax.optimization_barrier(jnp.sum(partial_tan.astype(jnp.bfloat16).astype(jnp.float32), axis=0))
        added = live_here[:, None] * gate_here[:, None] * piece
        added_tan = live_here[:, None] * (gtan_here[:, None] * piece + gate_here[:, None] * piece_tan)
        return ((moe.at[tokens_here].add(added), moe_tan.at[tokens_here].add(added_tan)), None)
    start = (jnp.zeros((TOKENS, D), jnp.float32), jnp.zeros((TOKENS, D), jnp.float32))
    (moe, moe_tan), unused = lax.scan(expert_step, start, (token_of, live, gate_of, gtan_of, up_pieces, down_whole))
    mixed = (state_f + moe).astype(jnp.bfloat16)
    mixed_tan = (stan_f + moe_tan).astype(jnp.bfloat16)
    return (mixed, mixed_tan)
```

```python
import functools

import jax
import jax.numpy as jnp
import numpy as np
from jax import lax
from jax.experimental import pallas as pl
from jax.experimental.pallas import tpu as pltpu
from jax.sharding import PartitionSpec as P

D = 3072
HD = 128
TOK = 128
HEADS_HERE = 3
WIDTH = HEADS_HERE * HD
QUARTER = 768
EXPERTS = 16
CAP = 20
USED = 2 * CAP
SLAB = 48
PAIR = 2 * USED
ROWS = 640
HALF = ROWS // 2
HIDDEN = 1536
EPS = 1e-06
FACTOR = HD ** (-0.5)
LOG2E = 1.4426950408889634
MIB = 2**20

BF = jnp.bfloat16
F32 = jnp.float32
MESH = pl.DeviceIdType.MESH
VMEM = pltpu.VMEM
NT = (((1,), (1,)), ((), ()))
TN = (((0,), (0,)), ((), ()))
NN = (((1,), (0,)), ((), ()))


def dot(a, b, dims=NN):
    return lax.dot_general(a, b, dims, preferred_element_type=F32)


def coords():
    c = lax.axis_index("ctx")
    e = lax.axis_index("exp")
    return c // 8, (c // 2) % 4, c % 2, e // 2, e % 2


def device(z, y, xh, xl, core):
    return (z * 8 + y * 2 + xh, xl * 2 + core)


def meet(peers):
    barrier = pltpu.get_barrier_semaphore()
    for peer in peers:
        pl.semaphore_signal(barrier, inc=1, device_id=peer, device_id_type=MESH)
    pl.semaphore_wait(barrier, len(peers))


def remote(src, dst, send, recv, peer):
    return pltpu.make_async_remote_copy(
        src_ref=src, dst_ref=dst, send_sem=send, recv_sem=recv, device_id=peer, device_id_type=MESH
    )


YX = [(a, b) for a in range(4) for b in range(2) if a or b]
ZY = [(a, b) for a in range(4) for b in range(4) if a or b]


def gather_kernel(q, qt, k, v, kt, vt, qg, qtg, kg, vg, ktg, vtg, ssem, rsem, lsem):
    z, y, xh, xl, co = coords()
    here = y * 2 + xh
    peers_z = [device((z + a) % 4, y, xh, xl, co) for a in (1, 3, 2)]
    peers_q = [device(z, (y + a) % 4, (xh + b) % 2, xl, co) for a, b in YX]
    meet(peers_z + peers_q)
    copies = []
    n = 0
    for peer in peers_z:
        for src, dst in ((k, kg), (kt, ktg), (v, vg), (vt, vtg)):
            copies.append(remote(src, dst.at[z], ssem.at[n], rsem.at[n], peer))
            copies[-1].start()
            n += 1
    for peer in peers_q:
        for src, dst in ((q, qg), (qt, qtg)):
            copies.append(remote(src, dst.at[here], ssem.at[n], rsem.at[n], peer))
            copies[-1].start()
            n += 1
    own = ((k, kg, z), (kt, ktg, z), (v, vg, z), (vt, vtg, z), (q, qg, here), (qt, qtg, here))
    for i, (src, dst, at) in enumerate(own):
        copies.append(pltpu.make_async_copy(src, dst.at[at], lsem.at[i]))
        copies[-1].start()
    for copy in copies:
        copy.wait()


def attend_kernel(q, qt, k, kt, v, vt, out, stats):
    rows = []
    for h in range(HEADS_HERE):
        c = slice(h * HD, (h + 1) * HD)
        qh, qth = q[:, :, c].reshape(256, HD), qt[:, :, c].reshape(256, HD)
        kh, kth = k[:, :, c].reshape(512, HD), kt[:, :, c].reshape(512, HD)
        vh, vth = v[:, :, c].reshape(512, HD), vt[:, :, c].reshape(512, HD)
        scores = dot(kh, qh, NT) * (FACTOR * LOG2E)
        tan = dot(jnp.concatenate([kh, kth], 1), jnp.concatenate([qth, qh], 1), NT) * FACTOR
        high = jnp.max(scores, axis=0, keepdims=True)
        weights = jnp.exp2(scores - high)
        total = jnp.sum(weights, axis=0, keepdims=True)
        weights = weights * (1.0 / total)
        mean = jnp.sum(weights * tan, axis=0, keepdims=True)
        tilted = (weights * (tan - mean)).astype(BF)
        both = dot(weights.astype(BF), jnp.concatenate([vh, vth], 1), TN)
        tout = both[:, HD:] + dot(tilted, vh, TN)
        out[:, :, c] = both[:, :HD].astype(BF).reshape(2, TOK, HD)
        out[:, :, WIDTH + h * HD : WIDTH + (h + 1) * HD] = tout.astype(BF).reshape(2, TOK, HD)
        rows.append((high + jnp.log2(total), mean))
    pad = jnp.zeros((2, 256), F32)
    table = jnp.concatenate([r[0] for r in rows] + [r[1] for r in rows] + [pad], axis=0)
    stats[0] = table[:, :TOK]
    stats[1] = table[:, TOK:]


def spread_tables():
    col = np.arange(EXPERTS * SLAB)
    row = col % SLAB
    slot = np.where(row < 16, row, np.where(row < 32, row - 16, np.where(row < 36, row - 16, row - 20)))
    slot = np.where(row < USED, slot, -1)
    tan = ((row >= 16) & (row < 32)) | ((row >= 36) & (row < USED))
    spread = (np.arange(EXPERTS)[:, None] == (col // SLAB)[None, :]).astype(np.float32)
    info = np.zeros((8, EXPERTS * SLAB), np.float32)
    info[0] = np.where(tan, -1, slot)
    info[1] = np.where(tan, slot, -1)
    return spread, info


def to_columns(rows):
    n = rows.shape[0]
    return jnp.concatenate([rows, jnp.zeros((128 - n, 128), F32)], axis=0).T


def middle_kernel(
    ot, stats, out_proj, res, rest, shift, scale, router, ids, spread, info,
    packed, state, ghi, glo,
    got, gstats, mine, sib, far, farin, mstat, gstat, mlog, glog, acc,
    s1, r1, s2, r2, s3, r3, s4, r4, s5, r5, lsem,
):
    z, y, xh, xl, co = coords()
    e = xl * 2 + co
    here = y * 2 + xh
    sibling = device(z, y, xh, xl, 1 - co)
    across = device(z, y, xh, 1 - xl, co)
    diagonal = device(z, y, xh, 1 - xl, 1 - co)
    peers_q = [device(z, (y + a) % 4, (xh + b) % 2, xl, co) for a, b in YX]
    peers_e = [sibling, across, diagonal]
    meet(peers_q + peers_e)
    first = []
    for n, ((a, b), peer) in enumerate(zip(YX, peers_q)):
        there = ((y + a) % 4) * 2 + (xh + b) % 2
        first.append(remote(stats.at[there], gstats.at[here], s2.at[n], r2.at[n], peer))
        first[-1].start()
        first.append(remote(ot.at[there], got.at[here], s1.at[n], r1.at[n], peer))
        first[-1].start()
    for i, (src, dst) in enumerate(((stats, gstats), (ot, got))):
        first.append(pltpu.make_async_copy(src.at[here], dst.at[here], lsem.at[i]))
        first[-1].start()

    expert = lax.broadcasted_iota(jnp.int32, (EXPERTS, TOK), 0)
    oh0 = (ids[0:1, :] == expert).astype(F32)
    oh1 = (ids[1:2, :] == expert).astype(F32)
    named = oh0 + oh1
    before = (
        lax.broadcasted_iota(jnp.int32, (TOK, TOK), 0) < lax.broadcasted_iota(jnp.int32, (TOK, TOK), 1)
    ).astype(BF)
    rank = dot(named.astype(BF), before)
    spread_b = spread[...]
    named_x = dot(named.astype(BF), spread_b, TN)
    rank_x = dot(rank.astype(BF), spread_b, TN)
    sel = jnp.where(rank_x == info[0:1, :], named_x, 0.0)
    selt = jnp.where(rank_x == info[1:2, :], named_x, 0.0)
    select = jnp.concatenate([sel, selt], axis=0).astype(BF)

    for copy in first:
        copy.wait()

    lse = [gstats[j, 0:3, :] for j in range(8)]
    mean = [gstats[j, 3:6, :] for j in range(8)]
    top = functools.reduce(jnp.maximum, lse)
    part = [jnp.exp2(item - top) for item in lse]
    inv = 1.0 / functools.reduce(jnp.add, part)
    part = [item * inv for item in part]
    mid = functools.reduce(jnp.add, [p * m for p, m in zip(part, mean)])
    lean = [p * (m - mid) for p, m in zip(part, mean)]
    cols = to_columns(jnp.concatenate(part + lean, axis=0))
    for h in range(HEADS_HERE):
        o = jnp.zeros((TOK, HD), F32)
        t = jnp.zeros((TOK, HD), F32)
        for j in range(8):
            oj = got[j, :, h * HD : (h + 1) * HD].astype(F32)
            tj = got[j, :, WIDTH + h * HD : WIDTH + (h + 1) * HD].astype(F32)
            w = cols[:, j * 3 + h : j * 3 + h + 1]
            c = cols[:, 24 + j * 3 + h : 24 + j * 3 + h + 1]
            o = o + w * oj
            t = t + w * tj + c * oj
        acc[0:TOK, h * HD : (h + 1) * HD] = o.astype(BF)
        acc[TOK:, h * HD : (h + 1) * HD] = t.astype(BF)

    att = acc[...]

    def project(xl_to, core_to):
        at = pl.multiple_of((xl_to * 2 + core_to) * QUARTER, QUARTER)
        return dot(att, out_proj[:, pl.ds(at, QUARTER)])

    mine[0] = project(1 - xl, 1 - co).astype(BF)
    to_sib0 = remote(mine.at[0], sib.at[0], s3.at[0], r3.at[0], sibling)
    to_sib0.start()
    mine[1] = project(xl, 1 - co).astype(BF)
    to_sib1 = remote(mine.at[1], sib.at[1], s3.at[1], r3.at[1], sibling)
    to_sib1.start()
    away = project(1 - xl, co)
    to_sib0.wait()
    far[...] = (away + sib[0].astype(F32)).astype(BF)
    to_far = remote(far, farin, s3.at[2], r3.at[2], across)
    to_far.start()
    kept = project(xl, co)
    to_sib1.wait()
    kept = kept + sib[1].astype(F32)
    to_far.wait()
    kept = kept + farin[...].astype(F32)
    st = (res[...].astype(F32) + kept[:TOK]).astype(BF)
    stt = (rest[...].astype(F32) + kept[TOK:]).astype(BF)
    state[0:TOK] = st
    state[TOK:] = stt
    sf = st.astype(F32)
    tf = stt.astype(F32)

    lane = lax.broadcasted_iota(jnp.int32, (TOK, 128), 1)
    sq = jnp.sum(sf * sf, axis=1, keepdims=True)
    cr = jnp.sum(sf * tf, axis=1, keepdims=True)
    mstat[...] = jnp.where(lane == 0, sq, jnp.where(lane == 1, cr, 0.0)).T[0:8]
    sends = []
    for n, peer in enumerate(peers_e):
        sends.append(remote(mstat, gstat.at[n], s4.at[n], r4.at[n], peer))
        sends[-1].start()
    for copy in sends:
        copy.wait()
    both = to_columns((mstat[...] + gstat[0]) + (gstat[1] + gstat[2])) * (1.0 / D)
    meansq, cross = both[:, 0:1], both[:, 1:2]
    recip = lax.rsqrt(meansq + EPS)
    gain = 1.0 + scale[pl.ds(e, 1), :]
    normed = (sf * recip * gain + shift[pl.ds(e, 1), :]).astype(BF)
    normed_tan = ((tf * recip - sf * (recip * recip * recip) * cross) * gain).astype(BF)
    rows = jnp.concatenate([normed, normed_tan], axis=0)

    mlog[...] = dot(router[e], rows, NT)
    sends = []
    for n, peer in enumerate(peers_e):
        sends.append(remote(mlog, glog.at[n], s5.at[n], r5.at[n], peer))
        sends[-1].start()
    for i in range(4):
        at = slice(i * 192, (i + 1) * 192)
        packed[i * 4 : (i + 1) * 4] = dot(select[:, at], rows, TN).astype(BF).reshape(4, SLAB, QUARTER)
    for copy in sends:
        copy.wait()

    logits = (mlog[...] + glog[0]) + (glog[1] + glog[2])
    ll, lt = logits[:, :TOK], logits[:, TOK:]
    own0 = jnp.sum(oh0 * ll, axis=0, keepdims=True)
    own1 = jnp.sum(oh1 * ll, axis=0, keepdims=True)
    diff = jnp.sum(oh0 * lt, axis=0, keepdims=True) - jnp.sum(oh1 * lt, axis=0, keepdims=True)
    gate0 = 1.0 / (1.0 + jnp.exp(own1 - own0))
    gate1 = 1.0 / (1.0 + jnp.exp(own0 - own1))
    gates = oh0 * gate0 + oh1 * gate1
    gates_tan = oh0 * (gate0 * (1.0 - gate0) * diff) - oh1 * (gate1 * (1.0 - gate1) * diff)
    ghigh = gates.astype(BF)
    glow = (gates - ghigh.astype(F32)).astype(BF)
    thigh = gates_tan.astype(BF)
    tlow = (gates_tan - thigh.astype(F32)).astype(BF)
    for ref, g, t in ((ghi, ghigh, thigh), (glo, glow, tlow)):
        gx = dot(g, spread_b, TN)
        tx = dot(t, spread_b, TN)
        ref[0:TOK] = (sel * gx).astype(BF)
        ref[TOK:] = (sel * tx + selt * gx).astype(BF)


def gelu_rows(v):
    n = v.shape[1]
    v = v.reshape(16, USED, n)
    p, t = v[:, 0:16].reshape(256, n), v[:, 16:32].reshape(256, n)
    mix = v[:, 32:40].reshape(128, n)
    low = lax.broadcasted_iota(jnp.int32, (128, n), 0) % 8 < 4
    u = jnp.where(low, mix, pltpu.roll(mix, 4, 0))

    def curves(x):
        sq = x * x
        th = jnp.tanh(0.7978845608028654 * x * (1.0 + 0.044715 * sq))
        half = 0.5 * (1.0 + th)
        slope = half + 0.5 * x * (1.0 - th * th) * (0.7978845608028654 * (1.0 + 0.134145 * sq))
        return x * half, slope

    g, s = curves(p)
    gm, sm = curves(u)
    m = jnp.where(low, gm, sm * mix)
    out = jnp.concatenate(
        [g.reshape(16, 16, n), (s * t).reshape(16, 16, n), m.reshape(16, 8, n)], axis=1
    )
    return out.reshape(ROWS, n).astype(BF)


def expert_kernel(
    packed, state, ghi, glo, up, down,
    mixed, mixed_tan,
    upv, downv, zin, x, pre, act, sibin, fwd_l, fwd_r, fin_l, fin_r, zout, zback,
    wsem, s1, r1, s2, r2, s3, r3, s4, r4, lsem,
):
    z, y, xh, xl, co = coords()
    pos = xh * 2 + xl
    here = z * 4 + y
    right, left, off = (pos + 1) % 4, (pos + 3) % 4, (pos + 2) % 4
    pair, other = xh * 2 + 1 - xl, (1 - xh) * 2 + 1 - xl

    def at_pos(p, c):
        return device(z, y, p // 2, p % 2, c)

    to_r, to_l, to_sib = at_pos(right, co), at_pos(left, co), at_pos(pos, 1 - co)
    peers = [device((z + a) % 4, (y + b) % 4, xh, xl, co) for a, b in ZY]
    load_up = pltpu.make_async_copy(up.at[0], upv, wsem.at[0])
    load_down = pltpu.make_async_copy(down.at[0], downv, wsem.at[1])
    meet(peers + [to_r, to_l, to_sib])

    moves = []
    for n, ((a, b), peer) in enumerate(zip(ZY, peers)):
        there = ((z + a) % 4) * 4 + (y + b) % 4
        moves.append(remote(packed.at[there], zin.at[here], s1.at[n], r1.at[n], peer))
        moves[-1].start()
    moves.append(pltpu.make_async_copy(packed.at[here], zin.at[here], lsem.at[0]))
    moves[-1].start()
    load_up.start()
    load_down.start()
    for copy in moves:
        copy.wait()
    block = pos * 2 + co

    def join(g, carry):
        a = zin[2 * g].astype(F32)[:USED]
        b = zin[2 * g + 1].astype(F32)[:USED]
        at = pl.multiple_of(g * PAIR, PAIR)
        x[block, pl.ds(at, PAIR), :] = jnp.concatenate([a, b], axis=0).astype(BF)
        return carry

    lax.fori_loop(0, 8, join, 0)

    def pass_on(n, b, half, peer):
        ref = x.at[b] if half is None else x.at[b, pl.ds(half * HALF, HALF)]
        return remote(ref, ref, s2.at[n], r2.at[n], peer)

    bl, br, bo = left * 2 + co, right * 2 + co, off * 2 + co
    c = [
        pass_on(0, block, None, to_sib),
        pass_on(1, block, 0, to_r),
        pass_on(2, block, 1, to_r),
        pass_on(3, block, 1, to_l),
        pass_on(4, block, 0, to_l),
        pass_on(5, bl, 0, to_r),
        pass_on(6, br, 1, to_l),
        pass_on(7, bl, 0, to_sib),
        pass_on(8, bl, 1, to_sib),
        pass_on(9, br, 0, to_sib),
        pass_on(10, br, 1, to_sib),
        pass_on(11, bo, 0, to_sib),
        pass_on(12, bo, 1, to_sib),
    ]
    for n in (1, 3, 0, 2, 4):
        c[n].start()

    def up_tile(p, n):
        cols = pl.ds(pl.multiple_of(n * 256, 256), 256)
        rows = pl.ds(pl.multiple_of((p % 2) * HIDDEN, HIDDEN), QUARTER)
        more = pl.ds(pl.multiple_of((p % 2) * HIDDEN + QUARTER, QUARTER), QUARTER)
        return dot(x[2 * p], upv[rows, cols]) + dot(x[2 * p + 1], upv[more, cols]), cols

    def up_first(p, at):
        def tile(n, carry):
            value, cols = up_tile(p, n)
            pre[at, :, cols] = value
            return carry

        lax.fori_loop(0, 6, tile, 0)

    def up_second(p, at):
        def tile(n, carry):
            value, cols = up_tile(p, n)
            act[at, :, cols] = gelu_rows(pre[at, :, cols] + value)
            return carry

        lax.fori_loop(0, 6, tile, 0)

    load_up.wait()
    c[0].wait_recv()
    up_first(pos, 0)
    c[1].wait_recv()
    c[5].start()
    c[7].start()
    c[3].wait_recv()
    c[6].start()
    c[10].start()
    c[2].wait_recv()
    c[8].start()
    c[4].wait_recv()
    c[9].start()
    for n in (7, 10, 8, 9):
        c[n].wait_recv()
    up_second(pair, 0)
    up_first(other, 1)
    c[5].wait_recv()
    c[11].start()
    c[6].wait_recv()
    c[12].start()
    c[11].wait_recv()
    c[12].wait_recv()
    up_second(off, 1)
    for copy in c:
        copy.wait_send()
    load_down.wait()

    def down_block(slot, p, core_to):
        at = jnp.where(p // 2 == xh, 0, 1)

        def tile(n, carry):
            first = ((p % 2) * 2 + core_to) * QUARTER
            cols = pl.ds(pl.multiple_of(first + n * 256, 256), 256)
            x[slot, :, pl.ds(pl.multiple_of(n * 256, 256), 256)] = dot(act[at], downv[:, cols]).astype(BF)
            return carry

        lax.fori_loop(0, 3, tile, 0)

    dests = (off, right, left, pos)
    sib = [remote(x.at[i], sibin.at[i], s3.at[i], r3.at[i], to_sib) for i in range(4)]

    def for_sib(i):
        down_block(i, dests[i], 1 - co)
        sib[i].start()

    def keep(i):
        down_block(4 + i, dests[i], co)

    def add(slot, half, *refs):
        at = pl.ds(half * HALF, HALF)

        def step(n, carry):
            rows = pl.ds(pl.multiple_of(half * HALF + n * 80, 80), 80)
            local = pl.ds(pl.multiple_of(n * 80, 80), 80)
            total = x[slot, rows].astype(F32)
            for ref in refs:
                total = total + (ref[rows] if ref.shape[0] == ROWS else ref[local]).astype(F32)
            x[slot, rows] = total.astype(BF)
            return carry

        lax.fori_loop(0, HALF // 80, step, 0)

    def ring(n, slot, half, dst, peer):
        return remote(x.at[slot, pl.ds(half * HALF, HALF)], dst, s3.at[n], r3.at[n], peer)

    top, low = pl.ds(0, HALF), pl.ds(HALF, HALF)
    off_r = ring(4, 4, 0, fwd_l, to_r)
    off_l = ring(5, 4, 1, fwd_r, to_l)
    r_low = ring(6, 5, 1, fin_l.at[low], to_r)
    r_top = ring(7, 5, 0, fin_l.at[top], to_r)
    l_top = ring(8, 6, 0, fin_r.at[top], to_l)
    l_low = ring(9, 6, 1, fin_r.at[low], to_l)

    for_sib(0)
    keep(0)
    for_sib(1)
    sib[0].wait_recv()
    add(4, 0, sibin.at[0])
    off_r.start()
    add(4, 1, sibin.at[0])
    off_l.start()
    keep(1)
    for_sib(2)
    sib[1].wait_recv()
    add(5, 1, sibin.at[1])
    r_low.start()
    keep(2)
    sib[2].wait_recv()
    add(6, 0, sibin.at[2])
    l_top.start()
    for_sib(3)
    keep(3)
    off_r.wait_recv()
    add(5, 0, sibin.at[1], fwd_l)
    r_top.start()
    off_l.wait_recv()
    add(6, 1, sibin.at[2], fwd_r)
    l_low.start()
    sib[3].wait_recv()
    for copy in (r_low, l_top, r_top, l_low):
        copy.wait_recv()

    def part(g, carry):
        rows = pl.ds(pl.multiple_of(g * PAIR, PAIR), PAIR)
        total = (x[7, rows].astype(F32) + sibin[3, rows].astype(F32)) + (
            fin_l[rows].astype(F32) + fin_r[rows].astype(F32)
        )
        blank = jnp.zeros((SLAB - USED, QUARTER), F32)
        zout[2 * g] = jnp.concatenate([total[:USED], blank], axis=0).astype(BF)
        zout[2 * g + 1] = jnp.concatenate([total[USED:], blank], axis=0).astype(BF)
        return carry

    lax.fori_loop(0, 8, part, 0)
    moves = []
    for n, ((a, b), peer) in enumerate(zip(ZY, peers)):
        there = ((z + a) % 4) * 4 + (y + b) % 4
        moves.append(remote(zout.at[there], zback.at[here], s4.at[n], r4.at[n], peer))
        moves[-1].start()
    moves.append(pltpu.make_async_copy(zout.at[here], zback.at[here], lsem.at[1]))
    moves[-1].start()
    for copy in sib + [off_r, off_l, r_low, r_top, l_top, l_low]:
        copy.wait_send()
    for copy in moves:
        copy.wait()
    back = zback[...].reshape(EXPERTS * SLAB, QUARTER)
    total = dot(ghi[...], back) + dot(glo[...], back) + state[...].astype(F32)
    mixed[...] = total[:TOK].astype(BF)
    mixed_tan[...] = total[TOK:].astype(BF)


def hbm(n):
    return [pl.BlockSpec(memory_space=pl.ANY)] * n


def vm(n):
    return [pl.BlockSpec(memory_space=VMEM)] * n


def params(cid, mib):
    return pltpu.CompilerParams(collective_id=cid, has_side_effects=True, vmem_limit_bytes=mib * MIB)


def sems(n):
    return pltpu.SemaphoreType.DMA((n,))


def shards(
    residual_in, residual_tan, queries, keys, values, query_tan, key_tan, value_tan,
    out_proj, shift_mod, scale_mod, router, up_weight, down_weight, expert_ids,
):
    shape = jax.ShapeDtypeStruct
    qs, ks = shape((8, TOK, WIDTH), BF), shape((4, TOK, WIDTH), BF)
    qg, qtg, kg, vg, ktg, vtg = pl.pallas_call(
        gather_kernel,
        out_shape=(qs, qs, ks, ks, ks, ks),
        in_specs=hbm(6),
        out_specs=tuple(hbm(6)),
        scratch_shapes=[sems(26), sems(26), sems(6)],
        compiler_params=params(1, 32),
        name="gather_rows",
    )(queries, query_tan, keys, values, key_tan, value_tan)

    two = pl.BlockSpec((2, TOK, WIDTH), lambda i: (i, 0, 0))
    all_keys = pl.BlockSpec((4, TOK, WIDTH), lambda i: (0, 0, 0))
    ot, stats = pl.pallas_call(
        attend_kernel,
        grid=(4,),
        out_shape=(shape((8, TOK, 2 * WIDTH), BF), shape((8, 8, TOK), F32)),
        in_specs=[two, two, all_keys, all_keys, all_keys, all_keys],
        out_specs=(
            pl.BlockSpec((2, TOK, 2 * WIDTH), lambda i: (i, 0, 0)),
            pl.BlockSpec((2, 8, TOK), lambda i: (i, 0, 0)),
        ),
        compiler_params=pltpu.CompilerParams(vmem_limit_bytes=48 * MIB),
        name="attend",
    )(qg, qtg, kg, ktg, vg, vtg)

    spread, info = spread_tables()
    slabs = shape((EXPERTS, SLAB, QUARTER), BF)
    wide = shape((2 * TOK, QUARTER), BF)
    packed, state, ghi, glo = pl.pallas_call(
        middle_kernel,
        out_shape=(slabs, wide, wide, wide),
        in_specs=vm(11),
        out_specs=tuple(vm(4)),
        scratch_shapes=[
            VMEM((8, TOK, 2 * WIDTH), BF),
            VMEM((8, 8, TOK), F32),
            VMEM((2, 2 * TOK, QUARTER), BF),
            VMEM((2, 2 * TOK, QUARTER), BF),
            VMEM((2 * TOK, QUARTER), BF),
            VMEM((2 * TOK, QUARTER), BF),
            VMEM((8, TOK), F32),
            VMEM((3, 8, TOK), F32),
            VMEM((EXPERTS, 2 * TOK), F32),
            VMEM((3, EXPERTS, 2 * TOK), F32),
            VMEM((2 * TOK, WIDTH), BF),
            sems(7), sems(7), sems(7), sems(7), sems(3), sems(3), sems(3), sems(3), sems(3), sems(3), sems(2),
        ],
        compiler_params=params(2, 48),
        name="project_and_pack",
    )(
        ot, stats, out_proj, residual_in, residual_tan,
        shift_mod.reshape(4, QUARTER), scale_mod.reshape(4, QUARTER),
        router.reshape(4, QUARTER, EXPERTS).transpose(0, 2, 1), expert_ids.T,
        jnp.asarray(spread, BF), jnp.asarray(info, F32),
    )

    out = shape((TOK, QUARTER), BF)
    half = VMEM((HALF, QUARTER), BF)
    whole = VMEM((ROWS, QUARTER), BF)
    slab = VMEM((EXPERTS, SLAB, QUARTER), BF)
    return pl.pallas_call(
        expert_kernel,
        out_shape=(out, out),
        in_specs=vm(4) + hbm(2),
        out_specs=tuple(vm(2)),
        scratch_shapes=[
            VMEM((D, HIDDEN), BF),
            VMEM((HIDDEN, D), BF),
            slab,
            VMEM((8, ROWS, QUARTER), BF),
            VMEM((2, ROWS, HIDDEN), F32),
            VMEM((2, ROWS, HIDDEN), BF),
            VMEM((4, ROWS, QUARTER), BF),
            half, half, whole, whole, slab, slab,
            sems(2), sems(15), sems(15), sems(13), sems(13), sems(10), sems(10), sems(15), sems(15), sems(2),
        ],
        compiler_params=params(3, 63),
        name="experts",
    )(packed, state, ghi, glo, up_weight, down_weight)


def solution(mesh):
    rows, heads = P("ctx", "exp"), P("exp", None)
    in_specs = (rows,) * 8 + (
        heads, P(), P(), P(), P("ctx", None, "exp"), P("ctx", "exp", None), P("ctx", None),
    )
    return jax.shard_map(shards, mesh=mesh, in_specs=in_specs, out_specs=(rows, rows), check_vma=False)
```

```python
import functools
import types

import jax
import jax.numpy as jnp
from jax import lax
from jax.experimental import pallas as pl
from jax.experimental.pallas import tpu as pltpu
from jax.sharding import PartitionSpec as P

D = 3072
HD = 128
TOK = 128
HEADS_HERE = 3
WIDTH = HEADS_HERE * HD
QUARTER = 768
EXPERTS = 16
CAP = 20
MAIN = 16
GROUP = 4 * CAP
ROWS = 640
HALF = ROWS // 2
COLS = QUARTER // 2
HIDDEN = 1536
EPS = 1e-06
FACTOR = HD ** (-0.5)
LOG2E = 1.4426950408889634
MIB = 2**20

BF = jnp.bfloat16
F32 = jnp.float32
MESH = pl.DeviceIdType.MESH
VMEM = pltpu.VMEM
NT = (((1,), (1,)), ((), ()))
TN = (((0,), (0,)), ((), ()))
NN = (((1,), (0,)), ((), ()))


def dot(a, b, dims=NN):
    return lax.dot_general(a, b, dims, preferred_element_type=F32)


def coords():
    c = lax.axis_index("ctx")
    e = lax.axis_index("exp")
    return c // 8, (c // 2) % 4, c % 2, e // 2, e % 2


def device(z, y, xh, xl, core):
    return (z * 8 + y * 2 + xh, xl * 2 + core)


def meet(peers):
    barrier = pltpu.get_barrier_semaphore()
    for peer in peers:
        pl.semaphore_signal(barrier, inc=1, device_id=peer, device_id_type=MESH)
    pl.semaphore_wait(barrier, len(peers))


def remote(src, dst, send, recv, peer):
    return pltpu.make_async_remote_copy(
        src_ref=src, dst_ref=dst, send_sem=send, recv_sem=recv, device_id=peer, device_id_type=MESH
    )


YX = [(0, 1)] + [(a, b) for a in (1, 3, 2) for b in (0, 1)]
ZY = [(a, b) for a in (2, 1, 3, 0) for b in (2, 1, 3, 0) if a or b]

INPUTS = (
    "q", "qt", "k", "v", "kt", "vt", "out_proj", "res", "rest", "up", "down", "router",
    "shift", "scale", "ids",
)
OUTPUTS = ("mixed", "mixed_tan")


def sems(n):
    return pltpu.SemaphoreType.DMA((n,))


SCRATCH = {
    "qg": VMEM((8, TOK, WIDTH), BF),
    "qtg": VMEM((8, TOK, WIDTH), BF),
    "kg": VMEM((4, TOK, WIDTH), BF),
    "ktg": VMEM((4, TOK, WIDTH), BF),
    "vg": VMEM((4, TOK, WIDTH), BF),
    "vtg": VMEM((4, TOK, WIDTH), BF),
    "ot": VMEM((2, 8, TOK, WIDTH), BF),
    "got": VMEM((2, 8, TOK, WIDTH), BF),
    "stats": VMEM((8, 8, TOK), F32),
    "gstats": VMEM((8, 8, TOK), F32),
    "proj": VMEM((WIDTH, D), BF),
    "state": VMEM((2, TOK, QUARTER), BF),
    "routerv": VMEM((EXPERTS, QUARTER), BF),
    "shiftv": VMEM((1, QUARTER), F32),
    "scalev": VMEM((1, QUARTER), F32),
    "idsv": VMEM((2, TOK), jnp.int32),
    "mine": VMEM((2, 2, TOK, QUARTER), BF),
    "sib": VMEM((2, 2, TOK, QUARTER), BF),
    "far": VMEM((2, TOK, QUARTER), BF),
    "farin": VMEM((2, TOK, QUARTER), BF),
    "mstat": VMEM((2, 8, TOK), F32),
    "gstat": VMEM((2, 3, 8, TOK), F32),
    "mlog": VMEM((EXPERTS, 2 * TOK), F32),
    "glog": VMEM((3, EXPERTS, 2 * TOK), F32),
    "acc": VMEM((2, TOK, WIDTH), BF),
    "kept": VMEM((TOK, QUARTER), F32),
    "normed": VMEM((2, TOK, QUARTER), BF),
    "gates": VMEM((4, 2 * TOK, 256), BF),
    "pmain": VMEM((2, EXPERTS, MAIN, QUARTER), BF),
    "prest": VMEM((2, EXPERTS, MAIN, 256), BF),
    "zrest": VMEM((2, EXPERTS, MAIN, 256), BF),
    "upv": VMEM((D, HIDDEN), BF),
    "downv": VMEM((HIDDEN, D), BF),
    "x": VMEM((8, ROWS, QUARTER), BF),
    "pre": VMEM((HALF, HIDDEN), F32),
    "slope": VMEM((2, HALF, HIDDEN), BF),
    "act": VMEM((2, 2, HALF, HIDDEN), BF),
    "down_out": VMEM((8, HALF, QUARTER), BF),
    "sibin": VMEM((2, 4, HALF, QUARTER), BF),
    "fwd_l": VMEM((2, HALF, COLS), BF),
    "fwd_r": VMEM((2, HALF, COLS), BF),
    "fin_l": VMEM((2, HALF, QUARTER), BF),
    "fin_r": VMEM((2, HALF, QUARTER), BF),
    "total": VMEM((2, HALF, QUARTER), BF),
    "trest": VMEM((2, EXPERTS, MAIN, 256), BF),
    "bmain": VMEM((2, EXPERTS, MAIN, QUARTER), BF),
    "brest": VMEM((2, EXPERTS, MAIN, 256), BF),
    "lsem": sems(27),
    "kv_s": sems(12), "kv_r": sems(12),
    "q_s": sems(16), "q_r": sems(16),
    "o_s": sems(24), "o_r": sems(24),
    "p_s": sems(6), "p_r": sems(6),
    "t_s": sems(6), "t_r": sems(6),
    "g_s": sems(3), "g_r": sems(3),
    "z_s": sems(60), "z_r": sems(60),
    "a_s": sems(22), "a_r": sems(22),
    "r_s": sems(20), "r_r": sems(20),
    "b_s": sems(60), "b_r": sems(60),
}


def to_columns(rows):
    n = rows.shape[0]
    return jnp.concatenate([rows, jnp.zeros((128 - n, 128), F32)], axis=0).T


def attend(r, yp):
    at = pl.ds(2 * yp, 2)
    for h in range(HEADS_HERE):
        c = slice(h * HD, (h + 1) * HD)
        qh, qth = r.qg[at, :, c].reshape(256, HD), r.qtg[at, :, c].reshape(256, HD)
        kh, kth = r.kg[:, :, c].reshape(512, HD), r.ktg[:, :, c].reshape(512, HD)
        vh, vth = r.vg[:, :, c].reshape(512, HD), r.vtg[:, :, c].reshape(512, HD)
        scores = dot(kh, qh, NT) * (FACTOR * LOG2E)
        tan = dot(jnp.concatenate([kh, kth], 1), jnp.concatenate([qth, qh], 1), NT) * FACTOR
        high = jnp.max(scores, axis=0, keepdims=True)
        weights = jnp.exp2(scores - high)
        total = jnp.sum(weights, axis=0, keepdims=True)
        weights = weights * (1.0 / total)
        mean = jnp.sum(weights * tan, axis=0, keepdims=True)
        tilted = (weights * (tan - mean)).astype(BF)
        both = dot(weights.astype(BF), jnp.concatenate([vh, vth], 1), TN)
        tout = both[:, HD:] + dot(tilted, vh, TN)
        r.ot[0, at, :, c] = both[:, :HD].astype(BF).reshape(2, TOK, HD)
        r.ot[1, at, :, c] = tout.astype(BF).reshape(2, TOK, HD)
        lse = high + jnp.log2(total)
        for i in range(2):
            part = slice(i * TOK, (i + 1) * TOK)
            r.stats[2 * yp + i, h : h + 1, :] = lse[:, part]
            r.stats[2 * yp + i, 4 + h : 5 + h, :] = mean[:, part]


def curves(x):
    sq = x * x
    th = jnp.tanh(0.7978845608028654 * x * (1.0 + 0.044715 * sq))
    half = 0.5 * (1.0 + th)
    slope = half + 0.5 * x * (1.0 - th * th) * (0.7978845608028654 * (1.0 + 0.134145 * sq))
    return x * half, slope


def block_kernel(*refs):
    r = types.SimpleNamespace(**dict(zip(INPUTS + OUTPUTS + tuple(SCRATCH), refs)))
    z, y, xh, xl, co = coords()
    e = xl * 2 + co
    pos = xh * 2 + xl
    here_q = y * 2 + xh
    here = z * 4 + y
    right, left, off = (pos + 1) % 4, (pos + 3) % 4, (pos + 2) % 4
    pair, other = xh * 2 + 1 - xl, (1 - xh) * 2 + 1 - xl

    def at_pos(p, c):
        return device(z, y, p // 2, p % 2, c)

    def near(a, b):
        return device(z, (y + a) % 4, (xh + b) % 2, xl, co)

    to_r, to_l, to_sib = at_pos(right, co), at_pos(left, co), at_pos(pos, 1 - co)
    across, diagonal = at_pos(pair, co), at_pos(pair, 1 - co)
    peers_e = [to_sib, across, diagonal]
    peers_zy = [device((z + a) % 4, (y + b) % 4, xh, xl, co) for a, b in ZY]
    meet(peers_zy + [near(a, 1) for a in range(4)] + peers_e + [at_pos(other, co)])

    kv = []
    for n, a in enumerate((1, 3, 2)):
        peer = device((z + a) % 4, y, xh, xl, co)
        for i, (src, dst) in enumerate(((r.k, r.kg), (r.kt, r.ktg), (r.v, r.vg), (r.vt, r.vtg))):
            kv.append(remote(src, dst.at[z], r.kv_s.at[n * 4 + i], r.kv_r.at[n * 4 + i], peer))
            kv[-1].start()

    def q_copies(a, b):
        n = 4 * a + 2 * b
        return [
            remote(src, dst.at[here_q], r.q_s.at[n + i], r.q_r.at[n + i], near(a, b))
            for i, (src, dst) in enumerate(((r.q, r.qg), (r.qt, r.qtg)))
        ]

    for a, b in YX:
        for copy in q_copies(a, b):
            copy.start()
    quarter = pl.ds(pl.multiple_of(e * QUARTER, QUARTER), QUARTER)
    local = [
        pltpu.make_async_copy(src, dst, r.lsem.at[i])
        for i, (src, dst) in enumerate(
            (
                (r.k, r.kg.at[z]), (r.kt, r.ktg.at[z]), (r.v, r.vg.at[z]), (r.vt, r.vtg.at[z]),
                (r.q, r.qg.at[here_q]), (r.qt, r.qtg.at[here_q]),
                (r.out_proj, r.proj), (r.res, r.state.at[0]), (r.rest, r.state.at[1]),
                (r.router.at[:, quarter], r.routerv),
                (r.shift.at[:, quarter], r.shiftv), (r.scale.at[:, quarter], r.scalev), (r.ids, r.idsv),
                (r.up.at[0], r.upv), (r.down.at[0], r.downv),
            )
        )
    ]
    for copy in local:
        copy.start()

    r.stats[...] = jnp.zeros_like(r.stats)
    local[12].wait()
    expert = lax.broadcasted_iota(jnp.int32, (EXPERTS, TOK), 0)
    oh0 = (r.idsv[0:1, :] == expert).astype(F32)
    oh1 = (r.idsv[1:2, :] == expert).astype(F32)
    named = (oh0 + oh1).astype(BF)

    def iota(shape, dim):
        return lax.broadcasted_iota(jnp.int32, shape, dim)

    before = (iota((TOK, TOK), 0) < iota((TOK, TOK), 1)).astype(BF)
    rank = dot(named, before).astype(BF)
    spread = (iota((EXPERTS, 256), 1) // MAIN == iota((EXPERTS, 256), 0)).astype(BF)

    def selection():
        named_x = dot(named, spread, TN)
        rank_x = dot(rank, spread, TN)
        slot = iota((TOK, 256), 1) % MAIN
        main = jnp.where(rank_x == slot.astype(F32), named_x, 0.0)
        rest = jnp.where(rank_x == (MAIN + slot % 4).astype(F32), named_x, 0.0)
        return main, rest, slot // 4

    def out_copies(a, b, part):
        n = 6 * a + 3 * b
        there = ((y + a) % 4) * 2 + (xh + b) % 2
        moves = [
            remote(
                r.ot.at[part, there], r.got.at[part, here_q], r.o_s.at[n + part], r.o_r.at[n + part], near(a, b)
            )
        ]
        if part == 0:
            moves.append(
                remote(r.stats.at[there], r.gstats.at[here_q], r.o_s.at[n + 2], r.o_r.at[n + 2], near(a, b))
            )
        return moves

    for copy in local[:6]:
        copy.wait()
    for copy in kv:
        copy.wait_recv()
    for copy in q_copies(0, 1):
        copy.wait_recv()
    attend(r, y)
    for copy in out_copies(0, 1, 0):
        copy.start()
    keep = [
        pltpu.make_async_copy(r.stats.at[here_q], r.gstats.at[here_q], r.lsem.at[23]),
        pltpu.make_async_copy(r.ot.at[0, here_q], r.got.at[0, here_q], r.lsem.at[24]),
        pltpu.make_async_copy(r.ot.at[1, here_q], r.got.at[1, here_q], r.lsem.at[25]),
    ]
    for copy in keep:
        copy.start()

    def attend_step(i, carry):
        a = 1 + 2 * i - 3 * (i // 2)
        for b in (0, 1):
            for copy in q_copies(a, b):
                copy.wait_recv()
        attend(r, (y + 4 - a) % 4)
        for b in (0, 1):
            for copy in out_copies(4 - a, b, 0):
                copy.start()
        return carry

    lax.fori_loop(0, 3, attend_step, 0)
    for a, b in YX:
        out_copies(a, b, 1)[0].start()
    for copy in kv:
        copy.wait_send()
    for a, b in YX:
        for copy in q_copies(a, b):
            copy.wait_send()
    for copy in local[6:12] + keep:
        copy.wait()
    for a, b in YX:
        for copy in out_copies(a, b, 0):
            copy.wait()

    lse = [r.gstats[j, 0:3, :] for j in range(8)]
    mean = [r.gstats[j, 4:7, :] for j in range(8)]
    top = functools.reduce(jnp.maximum, lse)
    part = [jnp.exp2(item - top) for item in lse]
    inv = 1.0 / functools.reduce(jnp.add, part)
    part = [item * inv for item in part]
    mid = functools.reduce(jnp.add, [p * m for p, m in zip(part, mean)])
    lean = [p * (m - mid) for p, m in zip(part, mean)]
    cols = to_columns(jnp.concatenate(part + lean, axis=0))

    def merge(pt):
        for h in range(HEADS_HERE):
            at = slice(h * HD, (h + 1) * HD)
            sum_ = jnp.zeros((TOK, HD), F32)
            for j in range(8):
                w = cols[:, j * 3 + h : j * 3 + h + 1]
                sum_ = sum_ + w * r.got[pt, j, :, at].astype(F32)
                if pt == 1:
                    c = cols[:, 24 + j * 3 + h : 24 + j * 3 + h + 1]
                    sum_ = sum_ + c * r.got[0, j, :, at].astype(F32)
            r.acc[pt, :, at] = sum_.astype(BF)

    def project(pt, xl_to, core_to):
        at = pl.multiple_of((xl_to * 2 + core_to) * QUARTER, QUARTER)
        return dot(r.acc[pt], r.proj[:, pl.ds(at, QUARTER)])

    def project_move(pt, n, src, dst, peer):
        return remote(src, dst, r.p_s.at[pt * 3 + n], r.p_r.at[pt * 3 + n], peer)

    to_sib0 = [project_move(pt, 0, r.mine.at[pt, 0], r.sib.at[pt, 0], to_sib) for pt in range(2)]
    to_sib1 = [project_move(pt, 1, r.mine.at[pt, 1], r.sib.at[pt, 1], to_sib) for pt in range(2)]
    to_far = [project_move(pt, 2, r.far.at[pt], r.farin.at[pt], across) for pt in range(2)]

    def start_projection(pt):
        r.mine[pt, 0] = project(pt, 1 - xl, 1 - co).astype(BF)
        to_sib0[pt].start()
        r.mine[pt, 1] = project(pt, xl, 1 - co).astype(BF)
        to_sib1[pt].start()
        away = project(pt, 1 - xl, co)
        to_sib0[pt].wait()
        r.far[pt] = (away + r.sib[pt, 0].astype(F32)).astype(BF)
        to_far[pt].start()
        kept = project(pt, xl, co)
        to_sib1[pt].wait()
        r.kept[...] = kept + r.sib[pt, 1].astype(F32) + r.state[pt].astype(F32)

    def end_projection(pt):
        to_far[pt].wait()
        r.state[pt] = (r.kept[...] + r.farin[pt].astype(F32)).astype(BF)

    def start_mean(pt):
        product = jnp.sum(r.state[0].astype(F32) * r.state[pt].astype(F32), axis=1, keepdims=True)
        r.mstat[pt] = jnp.broadcast_to(product, (TOK, 128)).T[0:8]
        moves = [
            remote(r.mstat.at[pt], r.gstat.at[pt, n], r.t_s.at[pt * 3 + n], r.t_r.at[pt * 3 + n], peer)
            for n, peer in enumerate(peers_e)
        ]
        for copy in moves:
            copy.start()
        return moves

    def end_mean(pt, moves):
        for copy in moves:
            copy.wait()
        rows = (r.mstat[pt] + r.gstat[pt, 0]) + (r.gstat[pt, 1] + r.gstat[pt, 2])
        return to_columns(rows)[:, 0:1] * (1.0 / D)

    block = pos * 2 + co

    def rows_of(source):
        return pl.ds(pl.multiple_of((source // 4) * GROUP + (source % 4) * MAIN, MAIN), MAIN)

    def x_rows_of(pt, source):
        return pl.ds(pl.multiple_of(pt * HALF + (source // 4) * GROUP + (source % 4) * MAIN, MAIN), MAIN)

    def plane(pt, main, rest, send, recv, lsem):
        moves = []
        for i, (src, dst) in enumerate((main, rest)):
            for n, ((a, b), peer) in enumerate(zip(ZY, peers_zy)):
                there = ((z + a) % 4) * 4 + (y + b) % 4
                at = pt * 30 + i * 15 + n
                moves.append(remote(src(there), dst(here), send.at[at], recv.at[at], peer))
            moves.append(pltpu.make_async_copy(src(here), dst(here), r.lsem.at[lsem + 2 * pt + i]))
        for copy in moves:
            copy.start()
        return moves

    def route(pt):
        main, rest, piece = selection()
        rows = r.normed[pt]
        r.pmain[pt] = dot(main.astype(BF), rows, TN).astype(BF).reshape(EXPERTS, MAIN, QUARTER)
        value = jnp.zeros((256, 256), F32)
        for g in range(3):
            chosen = jnp.where(piece == g, rest, 0.0).astype(BF)
            value = value + dot(chosen, rows[:, g * 256 : (g + 1) * 256], TN)
        r.prest[pt] = value.astype(BF).reshape(EXPERTS, MAIN, 256)
        return plane(
            pt,
            (lambda s: r.pmain.at[pt, s], lambda s: r.x.at[block, x_rows_of(pt, s)]),
            (lambda s: r.prest.at[pt, s], lambda s: r.zrest.at[pt, s]),
            r.z_s, r.z_r, 15,
        )

    def piece_rows(g):
        to, source = iota((64, 256), 0), iota((64, 256), 1)
        return ((to // 4 == source // MAIN) & (source % MAIN == 4 * g + to % 4)).astype(BF)

    def end_route(pt, moves):
        for copy in moves:
            copy.wait()
        rest = r.zrest[pt].reshape(256, 256)
        for g in range(3):
            value = dot(piece_rows(g), rest).astype(BF)
            for i in range(4):
                at = slice(pt * HALF + i * GROUP + 64, pt * HALF + (i + 1) * GROUP)
                r.x[block, at, g * 256 : (g + 1) * 256] = value[i * 16 : (i + 1) * 16]

    x = r.x
    bl, br, bo = left * 2 + co, right * 2 + co, off * 2 + co

    def half_cols(h):
        return pl.ds(h * COLS, COLS)

    def pass_on(pt, n, b, h, peer):
        cols = pl.ds(0, QUARTER) if h is None else half_cols(h)
        ref = x.at[b, pl.ds(pt * HALF, HALF), cols]
        return remote(ref, ref, r.a_s.at[pt * 11 + n], r.a_r.at[pt * 11 + n], peer)

    def ring_copies(pt):
        return types.SimpleNamespace(
            own=pass_on(pt, 0, block, None, to_sib),
            r0=pass_on(pt, 1, block, 0, to_r),
            r1=pass_on(pt, 2, block, 1, to_r),
            l1=pass_on(pt, 3, block, 1, to_l),
            l0=pass_on(pt, 4, block, 0, to_l),
            fr=pass_on(pt, 5, bl, 0, to_r),
            fl=pass_on(pt, 6, br, 1, to_l),
            sl=pass_on(pt, 7, bl, None, to_sib),
            sr=pass_on(pt, 8, br, None, to_sib),
            s0=pass_on(pt, 9, bo, 0, to_sib),
            s1=pass_on(pt, 10, bo, 1, to_sib),
        )

    spin = [ring_copies(pt) for pt in range(2)]

    def start_ring(pt):
        c = spin[pt]
        for copy in (c.r0, c.l1, c.r1, c.l0, c.own):
            copy.start()

    def forward_far(pt):
        c = spin[pt]
        c.r0.wait_recv()
        c.fr.start()
        c.l1.wait_recv()
        c.fl.start()

    def forward_near(pt):
        c = spin[pt]
        c.r1.wait_recv()
        c.sl.start()
        c.l0.wait_recv()
        c.sr.start()

    def end_ring(pt):
        c = spin[pt]
        c.fr.wait_recv()
        c.s0.start()
        c.fl.wait_recv()
        c.s1.start()

    def up_tile(pt, p, n):
        cols = pl.ds(pl.multiple_of(n * 512, 512), 512)
        a = pl.ds(pl.multiple_of((p % 2) * HIDDEN, HIDDEN), QUARTER)
        b = pl.ds(pl.multiple_of((p % 2) * HIDDEN + QUARTER, QUARTER), QUARTER)
        rows = slice(pt * HALF, (pt + 1) * HALF)
        return dot(x[2 * p, rows], r.upv[a, cols]) + dot(x[2 * p + 1, rows], r.upv[b, cols]), cols

    def up_first(pt, p):
        def tile(n, carry):
            value, cols = up_tile(pt, p, n)
            r.pre[:, cols] = value
            return carry

        lax.fori_loop(0, 3, tile, 0)

    def up_second(pt, p, at):
        def tile(n, carry):
            value, cols = up_tile(pt, p, n)
            value = r.pre[:, cols] + value
            if pt == 0:
                value, slope = curves(value)
                r.slope[at, :, cols] = slope.astype(BF)
            else:
                value = value * r.slope[at, :, cols].astype(F32)
            r.act[pt, at, :, cols] = value.astype(BF)
            return carry

        lax.fori_loop(0, 3, tile, 0)

    dests = (off, right, left, pos)

    def out_ref(pt, i):
        return r.down_out.at[i] if pt == 0 else x.at[i, pl.ds(0, HALF)]

    def down_part(pt, i, core_to):
        p = dests[i]
        at = jnp.where(p // 2 == xh, 0, 1)
        cols = pl.ds(pl.multiple_of(((p % 2) * 2 + core_to) * QUARTER, QUARTER), QUARTER)
        out_ref(pt, 2 * i + (0 if core_to is not co else 1))[...] = dot(r.act[pt, at], r.downv[:, cols]).astype(BF)

    def add(pt, i, h, *more):
        dst = out_ref(pt, 2 * i + 1)
        cols = slice(h * COLS, (h + 1) * COLS)

        def step(n, carry):
            at = pl.ds(pl.multiple_of(n * 80, 80), 80)
            value = dst[at, cols].astype(F32) + r.sibin[pt, i, at, cols].astype(F32)
            for ref in more:
                value = value + ref[pt, at].astype(F32)
            dst[at, cols] = value.astype(BF)
            return carry

        lax.fori_loop(0, HALF // 80, step, 0)

    def sum_copies(pt):
        def move(n, src, dst, peer):
            return remote(src, dst, r.r_s.at[pt * 10 + n], r.r_r.at[pt * 10 + n], peer)

        def piece(i, h):
            return out_ref(pt, 2 * i + 1).at[:, half_cols(h)]

        return types.SimpleNamespace(
            sib=[move(i, out_ref(pt, 2 * i), r.sibin.at[pt, i], to_sib) for i in range(4)],
            off_r=move(4, piece(0, 0), r.fwd_l.at[pt], to_r),
            off_l=move(5, piece(0, 1), r.fwd_r.at[pt], to_l),
            r0=move(6, piece(1, 0), r.fin_l.at[pt, :, half_cols(0)], to_r),
            r1=move(7, piece(1, 1), r.fin_l.at[pt, :, half_cols(1)], to_r),
            l0=move(8, piece(2, 0), r.fin_r.at[pt, :, half_cols(0)], to_l),
            l1=move(9, piece(2, 1), r.fin_r.at[pt, :, half_cols(1)], to_l),
        )

    sums = [sum_copies(pt) for pt in range(2)]

    def both_parts(pt, i):
        down_part(pt, i, 1 - co)
        sums[pt].sib[i].start()
        down_part(pt, i, co)

    def start_sums(pt):
        c = sums[pt]
        c.sib[0].wait_recv()
        add(pt, 0, 0)
        c.off_r.start()
        add(pt, 0, 1)
        c.off_l.start()

    def neighbour_sums(pt):
        c = sums[pt]
        c.sib[1].wait_recv()
        add(pt, 1, 1)
        c.r1.start()
        c.sib[2].wait_recv()
        add(pt, 2, 0)
        c.l0.start()

    def forward_sums(pt):
        c = sums[pt]
        c.off_r.wait_recv()
        add(pt, 1, 0, r.fwd_l)
        c.r0.start()
        c.off_l.wait_recv()
        add(pt, 2, 1, r.fwd_r)
        c.l1.start()

    def leave(pt):
        c = sums[pt]
        for copy in (c.sib[3], c.r1, c.l0, c.r0, c.l1):
            copy.wait_recv()
        own = out_ref(pt, 7)

        def step(g, carry):
            at = pl.ds(pl.multiple_of(g * GROUP, GROUP), GROUP)
            value = (own[at].astype(F32) + r.sibin[pt, 3, at].astype(F32)) + (
                r.fin_l[pt, at].astype(F32) + r.fin_r[pt, at].astype(F32)
            )
            r.total[pt, at] = value.astype(BF)
            return carry

        lax.fori_loop(0, 4, step, 0)
        rest = jnp.concatenate([r.total[pt, i * GROUP + 64 : (i + 1) * GROUP] for i in range(4)], axis=0)
        value = jnp.zeros((256, 256), F32)
        for g in range(3):
            value = value + dot(piece_rows(g), rest[:, g * 256 : (g + 1) * 256], TN)
        r.trest[pt] = value.astype(BF).reshape(EXPERTS, MAIN, 256)
        return plane(
            pt,
            (lambda s: r.total.at[pt, rows_of(s)], lambda s: r.bmain.at[pt, s]),
            (lambda s: r.trest.at[pt, s], lambda s: r.brest.at[pt, s]),
            r.b_s, r.b_r, 19,
        )

    merge(0)
    start_projection(0)
    end_projection(0)
    moves = start_mean(0)
    gain = 1.0 + r.scalev[...]
    recip = lax.rsqrt(end_mean(0, moves) + EPS)
    sf = r.state[0].astype(F32)
    r.normed[0] = (sf * recip * gain + r.shiftv[...]).astype(BF)
    route0 = route(0)

    for a, b in YX:
        out_copies(a, b, 1)[0].wait()
    merge(1)
    start_projection(1)
    end_route(0, route0)
    start_ring(0)
    end_projection(1)
    moves = start_mean(1)
    cross = end_mean(1, moves)
    sf, tf = r.state[0].astype(F32), r.state[1].astype(F32)
    r.normed[1] = ((tf * recip - sf * (recip * recip * recip) * cross) * gain).astype(BF)
    route1 = route(1)
    both = r.normed[...].reshape(2 * TOK, QUARTER)
    r.mlog[...] = dot(r.routerv[...], both, NT)
    log_moves = [
        remote(r.mlog, r.glog.at[n], r.g_s.at[n], r.g_r.at[n], peer) for n, peer in enumerate(peers_e)
    ]
    for copy in log_moves:
        copy.start()

    for copy in local[13:]:
        copy.wait()
    c0, c1 = spin
    c0.own.wait_recv()
    up_first(0, pos)
    forward_far(0)
    forward_near(0)
    end_route(1, route1)
    start_ring(1)
    c0.sl.wait_recv()
    c0.sr.wait_recv()
    up_second(0, pair, 0)
    end_ring(0)
    up_first(0, other)
    c0.s0.wait_recv()
    c0.s1.wait_recv()
    up_second(0, off, 1)
    both_parts(0, 0)
    forward_far(1)
    start_sums(0)
    forward_near(1)
    c1.own.wait_recv()
    up_first(1, pos)
    both_parts(0, 1)
    c1.sl.wait_recv()
    c1.sr.wait_recv()
    up_second(1, pair, 0)
    end_ring(1)
    both_parts(0, 2)
    neighbour_sums(0)
    forward_sums(0)
    up_first(1, other)
    c1.s0.wait_recv()
    c1.s1.wait_recv()
    up_second(1, off, 1)
    for c in spin:
        for copy in vars(c).values():
            copy.wait_send()
    both_parts(1, 0)
    both_parts(0, 3)
    start_sums(1)
    both_parts(1, 1)
    both_parts(1, 2)
    neighbour_sums(1)
    back0 = leave(0)
    forward_sums(1)
    both_parts(1, 3)

    for copy in log_moves:
        copy.wait()
    logits = (r.mlog[...] + r.glog[0]) + (r.glog[1] + r.glog[2])
    ll, lt = logits[:, :TOK], logits[:, TOK:]
    own0 = jnp.sum(oh0 * ll, axis=0, keepdims=True)
    own1 = jnp.sum(oh1 * ll, axis=0, keepdims=True)
    diff = jnp.sum(oh0 * lt, axis=0, keepdims=True) - jnp.sum(oh1 * lt, axis=0, keepdims=True)
    gate0 = 1.0 / (1.0 + jnp.exp(own1 - own0))
    gate1 = 1.0 / (1.0 + jnp.exp(own0 - own1))
    gates = oh0 * gate0 + oh1 * gate1
    gates_tan = oh0 * (gate0 * (1.0 - gate0) * diff) - oh1 * (gate1 * (1.0 - gate1) * diff)
    main, rest, piece = selection()
    for i, g in enumerate((gates, gates_tan)):
        high = g.astype(BF)
        low = (g - high.astype(F32)).astype(BF)
        at = slice(i * TOK, (i + 1) * TOK)
        for j, item in enumerate((high, low)):
            wide = dot(item, spread, TN)
            r.gates[j, at] = (main * wide).astype(BF)
            r.gates[2 + j, at] = (rest * wide).astype(BF)

    back1 = leave(1)
    for c in sums:
        for copy in c.sib + [c.off_r, c.off_l, c.r0, c.r1, c.l0, c.l1]:
            copy.wait_send()

    def gated(pt, lhs):
        out = []
        for g in range(3):
            value = jnp.zeros((lhs.stop - lhs.start, 256), F32)
            rows = r.bmain[pt, :, :, g * 256 : (g + 1) * 256].reshape(256, 256)
            rest = r.brest[pt].reshape(256, 256)
            mask = iota((lhs.stop - lhs.start, 256), 1) % MAIN // 4 == g
            for j in range(2):
                value = value + dot(r.gates[j, lhs], rows)
                value = value + dot(jnp.where(mask, r.gates[2 + j, lhs], jnp.zeros((), BF)), rest)
            out.append(value)
        return out

    for copy in back0:
        copy.wait()
    primal = gated(0, slice(0, 2 * TOK))
    for g in range(3):
        at = slice(g * 256, (g + 1) * 256)
        r.mixed[:, at] = (r.state[0, :, at].astype(F32) + primal[g][:TOK]).astype(BF)
        r.kept[:, at] = r.state[1, :, at].astype(F32) + primal[g][TOK:]
    for copy in back1:
        copy.wait()
    tangent = gated(1, slice(0, TOK))
    for g in range(3):
        at = slice(g * 256, (g + 1) * 256)
        r.mixed_tan[:, at] = (r.kept[:, at] + tangent[g]).astype(BF)


def shards(
    residual_in, residual_tan, queries, keys, values, query_tan, key_tan, value_tan,
    out_proj, shift_mod, scale_mod, router, up_weight, down_weight, expert_ids,
):
    out = jax.ShapeDtypeStruct((TOK, QUARTER), BF)
    return pl.pallas_call(
        block_kernel,
        out_shape=(out, out),
        in_specs=[pl.BlockSpec(memory_space=pl.ANY)] * 15,
        out_specs=(pl.BlockSpec(memory_space=VMEM),) * 2,
        scratch_shapes=list(SCRATCH.values()),
        compiler_params=pltpu.CompilerParams(
            collective_id=1, has_side_effects=True, vmem_limit_bytes=64 * MIB - 64 * 1024
        ),
        name="block",
    )(
        queries, query_tan, keys, values, key_tan, value_tan, out_proj, residual_in, residual_tan,
        up_weight, down_weight, router.T, shift_mod[None], scale_mod[None], expert_ids.T,
    )


def solution(mesh):
    rows, heads = P("ctx", "exp"), P("exp", None)
    in_specs = (rows,) * 8 + (
        heads, P(), P(), P(), P("ctx", None, "exp"), P("ctx", "exp", None), P("ctx", None),
    )
    return jax.shard_map(shards, mesh=mesh, in_specs=in_specs, out_specs=(rows, rows), check_vma=False)
```

```python
import functools
import types

import jax
import jax.numpy as jnp
from jax import lax
from jax.experimental import pallas as pl
from jax.experimental.pallas import tpu as pltpu
from jax.sharding import PartitionSpec as P

D = 3072
HD = 128
TOK = 128
HEADS_HERE = 3
WIDTH = HEADS_HERE * HD
QUARTER = 768
EXPERTS = 16
CAP = 20
MAIN = 16
GROUP = 4 * CAP
ROWS = 640
HALF = ROWS // 2
COLS = QUARTER // 2
HIDDEN = 1536
EPS = 1e-06
FACTOR = HD ** (-0.5)
LOG2E = 1.4426950408889634
MIB = 2**20

BF = jnp.bfloat16
F32 = jnp.float32
MESH = pl.DeviceIdType.MESH
VMEM = pltpu.VMEM
NT = (((1,), (1,)), ((), ()))
TN = (((0,), (0,)), ((), ()))
NN = (((1,), (0,)), ((), ()))


def dot(a, b, dims=NN):
    return lax.dot_general(a, b, dims, preferred_element_type=F32)


def coords():
    c = lax.axis_index("ctx")
    e = lax.axis_index("exp")
    return c // 8, (c // 2) % 4, c % 2, e // 2, e % 2


def device(z, y, xh, xl, core):
    return (z * 8 + y * 2 + xh, xl * 2 + core)


def meet(peers):
    barrier = pltpu.get_barrier_semaphore()
    for peer in peers:
        pl.semaphore_signal(barrier, inc=1, device_id=peer, device_id_type=MESH)
    pl.semaphore_wait(barrier, len(peers))


def remote(src, dst, send, recv, peer):
    return pltpu.make_async_remote_copy(
        src_ref=src, dst_ref=dst, send_sem=send, recv_sem=recv, device_id=peer, device_id_type=MESH
    )


YX = [(0, 1)] + [(a, b) for a in (1, 3, 2) for b in (0, 1)]
ZY = [(a, b) for a in (2, 1, 3, 0) for b in (2, 1, 3, 0) if a or b]

INPUTS = (
    "q", "qt", "k", "v", "kt", "vt", "out_proj", "res", "rest", "up", "down", "router",
    "shift", "scale", "ids",
)
OUTPUTS = ("mixed", "mixed_tan")


def sems(n):
    return pltpu.SemaphoreType.DMA((n,))


SCRATCH = {
    "qg": VMEM((8, TOK, WIDTH), BF),
    "qtg": VMEM((8, TOK, WIDTH), BF),
    "kg": VMEM((4, TOK, WIDTH), BF),
    "ktg": VMEM((4, TOK, WIDTH), BF),
    "vg": VMEM((4, TOK, WIDTH), BF),
    "vtg": VMEM((4, TOK, WIDTH), BF),
    "ot": VMEM((2, 8, TOK, WIDTH), BF),
    "got": VMEM((2, 8, TOK, WIDTH), BF),
    "stats": VMEM((8, 8, TOK), F32),
    "gstats": VMEM((8, 8, TOK), F32),
    "proj": VMEM((WIDTH, D), BF),
    "state": VMEM((2, TOK, QUARTER), BF),
    "routerv": VMEM((EXPERTS, QUARTER), BF),
    "shiftv": VMEM((1, QUARTER), F32),
    "scalev": VMEM((1, QUARTER), F32),
    "idsv": VMEM((2, TOK), jnp.int32),
    "mine": VMEM((2, 2, TOK, QUARTER), BF),
    "sib": VMEM((2, 2, TOK, QUARTER), BF),
    "far": VMEM((2, TOK, QUARTER), BF),
    "farin": VMEM((2, TOK, QUARTER), BF),
    "mstat": VMEM((2, 8, TOK), F32),
    "gstat": VMEM((2, 3, 8, TOK), F32),
    "mlog": VMEM((EXPERTS, 2 * TOK), F32),
    "glog": VMEM((3, EXPERTS, 2 * TOK), F32),
    "acc": VMEM((2, TOK, WIDTH), BF),
    "kept": VMEM((TOK, QUARTER), F32),
    "normed": VMEM((2, TOK, QUARTER), BF),
    "gates": VMEM((4, 2 * TOK, 256), BF),
    "sel": VMEM((4, TOK, 256), BF),
    "pmain": VMEM((2, EXPERTS, MAIN, QUARTER), BF),
    "prest": VMEM((2, EXPERTS, MAIN, 256), BF),
    "zrest": VMEM((2, EXPERTS, MAIN, 256), BF),
    "upv": VMEM((D, HIDDEN), BF),
    "downv": VMEM((HIDDEN, D), BF),
    "x": VMEM((8, ROWS, QUARTER), BF),
    "pre": VMEM((HALF, HIDDEN), F32),
    "slope": VMEM((2, HALF, HIDDEN), BF),
    "act": VMEM((2, 2, HALF, HIDDEN), BF),
    "down_out": VMEM((8, HALF, QUARTER), BF),
    "sibin": VMEM((2, 4, HALF, QUARTER), BF),
    "fwd_l": VMEM((2, HALF, COLS), BF),
    "fwd_r": VMEM((2, HALF, COLS), BF),
    "fin_l": VMEM((2, HALF, QUARTER), BF),
    "fin_r": VMEM((2, HALF, QUARTER), BF),
    "total": VMEM((2, HALF, QUARTER), BF),
    "trest": VMEM((2, EXPERTS, MAIN, 256), BF),
    "bmain": VMEM((2, EXPERTS, MAIN, QUARTER), BF),
    "brest": VMEM((2, EXPERTS, MAIN, 256), BF),
    "lsem": sems(27),
    "kv_s": sems(12), "kv_r": sems(12),
    "q_s": sems(16), "q_r": sems(16),
    "o_s": sems(24), "o_r": sems(24),
    "p_s": sems(6), "p_r": sems(6),
    "t_s": sems(6), "t_r": sems(6),
    "g_s": sems(3), "g_r": sems(3),
    "z_s": sems(60), "z_r": sems(60),
    "a_s": sems(22), "a_r": sems(22),
    "r_s": sems(20), "r_r": sems(20),
    "b_s": sems(60), "b_r": sems(60),
}


def to_columns(rows):
    n = rows.shape[0]
    return jnp.concatenate([rows, jnp.zeros((128 - n, 128), F32)], axis=0).T


def attend(r, yp):
    at = pl.ds(2 * yp, 2)
    for h in range(HEADS_HERE):
        c = slice(h * HD, (h + 1) * HD)
        qh, qth = r.qg[at, :, c].reshape(256, HD), r.qtg[at, :, c].reshape(256, HD)
        kh, kth = r.kg[:, :, c].reshape(512, HD), r.ktg[:, :, c].reshape(512, HD)
        vh, vth = r.vg[:, :, c].reshape(512, HD), r.vtg[:, :, c].reshape(512, HD)
        scores = dot(kh, qh, NT) * (FACTOR * LOG2E)
        tan = dot(jnp.concatenate([kh, kth], 1), jnp.concatenate([qth, qh], 1), NT) * FACTOR
        high = jnp.max(scores, axis=0, keepdims=True)
        weights = jnp.exp2(scores - high)
        total = jnp.sum(weights, axis=0, keepdims=True)
        weights = weights * (1.0 / total)
        mean = jnp.sum(weights * tan, axis=0, keepdims=True)
        tilted = (weights * (tan - mean)).astype(BF)
        both = dot(weights.astype(BF), jnp.concatenate([vh, vth], 1), TN)
        tout = both[:, HD:] + dot(tilted, vh, TN)
        r.ot[0, at, :, c] = both[:, :HD].astype(BF).reshape(2, TOK, HD)
        r.ot[1, at, :, c] = tout.astype(BF).reshape(2, TOK, HD)
        lse = high + jnp.log2(total)
        for i in range(2):
            part = slice(i * TOK, (i + 1) * TOK)
            r.stats[2 * yp + i, h : h + 1, :] = lse[:, part]
            r.stats[2 * yp + i, 4 + h : 5 + h, :] = mean[:, part]


def curves(x):
    sq = x * x
    th = jnp.tanh(0.7978845608028654 * x * (1.0 + 0.044715 * sq))
    half = 0.5 * (1.0 + th)
    slope = half + 0.5 * x * (1.0 - th * th) * (0.7978845608028654 * (1.0 + 0.134145 * sq))
    return x * half, slope


def block_kernel(*refs):
    r = types.SimpleNamespace(**dict(zip(INPUTS + OUTPUTS + tuple(SCRATCH), refs)))
    z, y, xh, xl, co = coords()
    e = xl * 2 + co
    pos = xh * 2 + xl
    here_q = y * 2 + xh
    here = z * 4 + y
    right, left, off = (pos + 1) % 4, (pos + 3) % 4, (pos + 2) % 4
    pair, other = xh * 2 + 1 - xl, (1 - xh) * 2 + 1 - xl

    def at_pos(p, c):
        return device(z, y, p // 2, p % 2, c)

    def near(a, b):
        return device(z, (y + a) % 4, (xh + b) % 2, xl, co)

    to_r, to_l, to_sib = at_pos(right, co), at_pos(left, co), at_pos(pos, 1 - co)
    across, diagonal = at_pos(pair, co), at_pos(pair, 1 - co)
    peers_e = [to_sib, across, diagonal]
    peers_zy = [device((z + a) % 4, (y + b) % 4, xh, xl, co) for a, b in ZY]
    meet(peers_zy + [near(a, 1) for a in range(4)] + peers_e + [at_pos(other, co)])

    z_up, z_down = device((z + 1) % 4, y, xh, xl, co), device((z + 3) % 4, y, xh, xl, co)
    y_up, y_down = near(1, 0), near(3, 0)

    def kv_copy(n, src, dst, at, peer):
        return remote(src, dst.at[at], r.kv_s.at[n], r.kv_r.at[n], peer)

    kv_pairs = ((r.k, r.kg), (r.kt, r.ktg), (r.v, r.vg), (r.vt, r.vtg))
    kv_up = [kv_copy(i, src, dst, z, z_up) for i, (src, dst) in enumerate(kv_pairs)]
    kv_down = [kv_copy(4 + i, src, dst, z, z_down) for i, (src, dst) in enumerate(kv_pairs)]
    z_before, z_after = (z + 3) % 4, (z + 1) % 4
    kv_on = [
        kv_copy(8, r.kg.at[z_before], r.kg, z_before, z_up),
        kv_copy(9, r.ktg.at[z_before], r.ktg, z_before, z_up),
        kv_copy(10, r.vg.at[z_after], r.vg, z_after, z_down),
        kv_copy(11, r.vtg.at[z_after], r.vtg, z_after, z_down),
    ]

    def q_copy(n, src, dst, at, peer):
        return remote(src, dst.at[at], r.q_s.at[n], r.q_r.at[n], peer)

    q_pairs = ((r.q, r.qg), (r.qt, r.qtg))
    q_over = [q_copy(i, src, dst, here_q, near(0, 1)) for i, (src, dst) in enumerate(q_pairs)]
    there_q = y * 2 + 1 - xh

    def q_round(n, sources, side):
        mine = y * 2 + side
        low, high = ((y + 3) % 4) * 2 + side, ((y + 1) % 4) * 2 + side
        up = [q_copy(n + i, src, dst, mine, y_up) for i, (src, dst) in enumerate(zip(sources, (r.qg, r.qtg)))]
        down = [q_copy(n + 2 + i, src, dst, mine, y_down) for i, (src, dst) in enumerate(zip(sources, (r.qg, r.qtg)))]
        on = [
            q_copy(n + 4, r.qg.at[low], r.qg, low, y_up),
            q_copy(n + 5, r.qtg.at[high], r.qtg, high, y_down),
        ]
        return up, down, on

    q_own = q_round(2, (r.q, r.qt), xh)
    q_other = q_round(8, (r.qg.at[there_q], r.qtg.at[there_q]), 1 - xh)

    def start_round(group):
        up, down, on = group
        for copy in (up[0], down[1], up[1], down[0]):
            copy.start()

    def pass_round(group):
        up, down, on = group
        up[0].wait_recv()
        on[0].start()
        down[1].wait_recv()
        on[1].start()

    for n in (0, 1):
        q_over[n].start()
        kv_up[n].start()
        kv_down[2 + n].start()
    start_round(q_own)
    for n in (0, 1):
        kv_up[2 + n].start()
        kv_down[n].start()
    kv = kv_up + kv_down + kv_on
    queries = q_over + [copy for group in q_own + q_other for copy in group]
    quarter = pl.ds(pl.multiple_of(e * QUARTER, QUARTER), QUARTER)
    local = [
        pltpu.make_async_copy(src, dst, r.lsem.at[i])
        for i, (src, dst) in enumerate(
            (
                (r.k, r.kg.at[z]), (r.kt, r.ktg.at[z]), (r.v, r.vg.at[z]), (r.vt, r.vtg.at[z]),
                (r.q, r.qg.at[here_q]), (r.qt, r.qtg.at[here_q]),
                (r.out_proj, r.proj), (r.res, r.state.at[0]), (r.rest, r.state.at[1]),
                (r.router.at[:, quarter], r.routerv),
                (r.shift.at[:, quarter], r.shiftv), (r.scale.at[:, quarter], r.scalev), (r.ids, r.idsv),
                (r.up.at[0], r.upv), (r.down.at[0], r.downv),
            )
        )
    ]
    for copy in local:
        copy.start()

    r.stats[...] = jnp.zeros_like(r.stats)
    local[12].wait()
    expert = lax.broadcasted_iota(jnp.int32, (EXPERTS, TOK), 0)
    oh0 = (r.idsv[0:1, :] == expert).astype(F32)
    oh1 = (r.idsv[1:2, :] == expert).astype(F32)
    named = (oh0 + oh1).astype(BF)

    def iota(shape, dim):
        return lax.broadcasted_iota(jnp.int32, shape, dim)

    before = (iota((TOK, TOK), 0) < iota((TOK, TOK), 1)).astype(BF)
    rank = dot(named, before).astype(BF)
    spread = (iota((EXPERTS, 256), 1) // MAIN == iota((EXPERTS, 256), 0)).astype(BF)

    named_x = dot(named, spread, TN)
    rank_x = dot(rank, spread, TN)
    slot = iota((TOK, 256), 1) % MAIN
    r.sel[0] = jnp.where(rank_x == slot.astype(F32), named_x, 0.0).astype(BF)
    extra = jnp.where(rank_x == (MAIN + slot % 4).astype(F32), named_x, 0.0)
    for g in range(3):
        r.sel[1 + g] = jnp.where(slot // 4 == g, extra, 0.0).astype(BF)

    def out_copies(a, b, part):
        n = 6 * a + 3 * b
        there = ((y + a) % 4) * 2 + (xh + b) % 2
        moves = [
            remote(
                r.ot.at[part, there], r.got.at[part, here_q], r.o_s.at[n + part], r.o_r.at[n + part], near(a, b)
            )
        ]
        if part == 0:
            moves.append(
                remote(r.stats.at[there], r.gstats.at[here_q], r.o_s.at[n + 2], r.o_r.at[n + 2], near(a, b))
            )
        return moves

    for copy in q_over:
        copy.wait_recv()
    start_round(q_other)
    for n in (0, 1):
        kv_up[n].wait_recv()
        kv_on[n].start()
        kv_down[2 + n].wait_recv()
        kv_on[2 + n].start()
    pass_round(q_own)
    pass_round(q_other)
    for copy in local[:6]:
        copy.wait()
    for copy in kv_up[2:] + kv_down[:2] + kv_on:
        copy.wait_recv()
    for up, down, on in (q_own, q_other):
        for copy in (up[1], down[0], on[0], on[1]):
            copy.wait_recv()
    attend(r, y)
    for copy in out_copies(0, 1, 0):
        copy.start()
    keep = [
        pltpu.make_async_copy(r.stats.at[here_q], r.gstats.at[here_q], r.lsem.at[23]),
        pltpu.make_async_copy(r.ot.at[0, here_q], r.got.at[0, here_q], r.lsem.at[24]),
        pltpu.make_async_copy(r.ot.at[1, here_q], r.got.at[1, here_q], r.lsem.at[25]),
    ]
    for copy in keep:
        copy.start()

    def attend_step(i, carry):
        a = 1 + 2 * i - 3 * (i // 2)
        attend(r, (y + 4 - a) % 4)
        for b in (0, 1):
            for copy in out_copies(4 - a, b, 0):
                copy.start()
        return carry

    lax.fori_loop(0, 3, attend_step, 0)
    for a, b in YX:
        out_copies(a, b, 1)[0].start()
    for copy in kv:
        copy.wait_send()
    for copy in queries:
        copy.wait_send()
    for copy in local[6:12] + keep:
        copy.wait()
    for a, b in YX:
        for copy in out_copies(a, b, 0):
            copy.wait()

    lse = [r.gstats[j, 0:3, :] for j in range(8)]
    mean = [r.gstats[j, 4:7, :] for j in range(8)]
    top = functools.reduce(jnp.maximum, lse)
    part = [jnp.exp2(item - top) for item in lse]
    inv = 1.0 / functools.reduce(jnp.add, part)
    part = [item * inv for item in part]
    mid = functools.reduce(jnp.add, [p * m for p, m in zip(part, mean)])
    lean = [p * (m - mid) for p, m in zip(part, mean)]
    cols = to_columns(jnp.concatenate(part + lean, axis=0))

    def merge(pt):
        for h in range(HEADS_HERE):
            at = slice(h * HD, (h + 1) * HD)
            sum_ = jnp.zeros((TOK, HD), F32)
            for j in range(8):
                w = cols[:, j * 3 + h : j * 3 + h + 1]
                sum_ = sum_ + w * r.got[pt, j, :, at].astype(F32)
                if pt == 1:
                    c = cols[:, 24 + j * 3 + h : 24 + j * 3 + h + 1]
                    sum_ = sum_ + c * r.got[0, j, :, at].astype(F32)
            r.acc[pt, :, at] = sum_.astype(BF)

    def project(pt, xl_to, core_to):
        at = pl.multiple_of((xl_to * 2 + core_to) * QUARTER, QUARTER)
        return dot(r.acc[pt], r.proj[:, pl.ds(at, QUARTER)])

    def project_move(pt, n, src, dst, peer):
        return remote(src, dst, r.p_s.at[pt * 3 + n], r.p_r.at[pt * 3 + n], peer)

    to_sib0 = [project_move(pt, 0, r.mine.at[pt, 0], r.sib.at[pt, 0], to_sib) for pt in range(2)]
    to_sib1 = [project_move(pt, 1, r.mine.at[pt, 1], r.sib.at[pt, 1], to_sib) for pt in range(2)]
    to_far = [project_move(pt, 2, r.far.at[pt], r.farin.at[pt], across) for pt in range(2)]

    def start_projection(pt):
        r.mine[pt, 0] = project(pt, 1 - xl, 1 - co).astype(BF)
        to_sib0[pt].start()
        r.mine[pt, 1] = project(pt, xl, 1 - co).astype(BF)
        to_sib1[pt].start()
        away = project(pt, 1 - xl, co)
        to_sib0[pt].wait()
        r.far[pt] = (away + r.sib[pt, 0].astype(F32)).astype(BF)
        to_far[pt].start()
        kept = project(pt, xl, co)
        to_sib1[pt].wait()
        r.kept[...] = kept + r.sib[pt, 1].astype(F32) + r.state[pt].astype(F32)

    def end_projection(pt):
        to_far[pt].wait()
        r.state[pt] = (r.kept[...] + r.farin[pt].astype(F32)).astype(BF)

    def start_mean(pt):
        product = jnp.sum(r.state[0].astype(F32) * r.state[pt].astype(F32), axis=1, keepdims=True)
        r.mstat[pt] = jnp.broadcast_to(product, (TOK, 128)).T[0:8]
        moves = [
            remote(r.mstat.at[pt], r.gstat.at[pt, n], r.t_s.at[pt * 3 + n], r.t_r.at[pt * 3 + n], peer)
            for n, peer in enumerate(peers_e)
        ]
        for copy in moves:
            copy.start()
        return moves

    def end_mean(pt, moves):
        for copy in moves:
            copy.wait()
        rows = (r.mstat[pt] + r.gstat[pt, 0]) + (r.gstat[pt, 1] + r.gstat[pt, 2])
        return to_columns(rows)[:, 0:1] * (1.0 / D)

    block = pos * 2 + co

    def rows_of(source):
        return pl.ds(pl.multiple_of((source // 4) * GROUP + (source % 4) * MAIN, MAIN), MAIN)

    def x_rows_of(pt, source):
        return pl.ds(pl.multiple_of(pt * HALF + (source // 4) * GROUP + (source % 4) * MAIN, MAIN), MAIN)

    def plane(pt, i, src, dst, send, recv, lsem):
        moves = []
        for n, ((a, b), peer) in enumerate(zip(ZY, peers_zy)):
            there = ((z + a) % 4) * 4 + (y + b) % 4
            at = pt * 30 + i * 15 + n
            moves.append(remote(src(there), dst(here), send.at[at], recv.at[at], peer))
        moves.append(pltpu.make_async_copy(src(here), dst(here), r.lsem.at[lsem + 2 * pt + i]))
        for copy in moves:
            copy.start()
        return moves

    def route(pt):
        rows = r.normed[pt]
        r.pmain[pt] = dot(r.sel[0], rows, TN).astype(BF).reshape(EXPERTS, MAIN, QUARTER)
        moves = plane(
            pt, 0, lambda s: r.pmain.at[pt, s], lambda s: r.x.at[block, x_rows_of(pt, s)], r.z_s, r.z_r, 15
        )
        value = jnp.zeros((256, 256), F32)
        for g in range(3):
            value = value + dot(r.sel[1 + g], rows[:, g * 256 : (g + 1) * 256], TN)
        r.prest[pt] = value.astype(BF).reshape(EXPERTS, MAIN, 256)
        return moves + plane(
            pt, 1, lambda s: r.prest.at[pt, s], lambda s: r.zrest.at[pt, s], r.z_s, r.z_r, 15
        )

    def piece_rows(g):
        to, source = iota((64, 256), 0), iota((64, 256), 1)
        return ((to // 4 == source // MAIN) & (source % MAIN == 4 * g + to % 4)).astype(BF)

    def end_route(pt, moves):
        for copy in moves:
            copy.wait()
        rest = r.zrest[pt].reshape(256, 256)
        for g in range(3):
            value = dot(piece_rows(g), rest).astype(BF)
            for i in range(4):
                at = slice(pt * HALF + i * GROUP + 64, pt * HALF + (i + 1) * GROUP)
                r.x[block, at, g * 256 : (g + 1) * 256] = value[i * 16 : (i + 1) * 16]

    x = r.x
    bl, br, bo = left * 2 + co, right * 2 + co, off * 2 + co

    def half_cols(h):
        return pl.ds(h * COLS, COLS)

    def pass_on(pt, n, b, h, peer):
        cols = pl.ds(0, QUARTER) if h is None else half_cols(h)
        ref = x.at[b, pl.ds(pt * HALF, HALF), cols]
        return remote(ref, ref, r.a_s.at[pt * 11 + n], r.a_r.at[pt * 11 + n], peer)

    def ring_copies(pt):
        return types.SimpleNamespace(
            own=pass_on(pt, 0, block, None, to_sib),
            r0=pass_on(pt, 1, block, 0, to_r),
            r1=pass_on(pt, 2, block, 1, to_r),
            l1=pass_on(pt, 3, block, 1, to_l),
            l0=pass_on(pt, 4, block, 0, to_l),
            fr=pass_on(pt, 5, bl, 0, to_r),
            fl=pass_on(pt, 6, br, 1, to_l),
            sl=pass_on(pt, 7, bl, None, to_sib),
            sr=pass_on(pt, 8, br, None, to_sib),
            s0=pass_on(pt, 9, bo, 0, to_sib),
            s1=pass_on(pt, 10, bo, 1, to_sib),
        )

    spin = [ring_copies(pt) for pt in range(2)]

    def start_ring(pt):
        c = spin[pt]
        for copy in (c.r0, c.l1, c.r1, c.l0, c.own):
            copy.start()

    def forward_far(pt):
        c = spin[pt]
        c.r0.wait_recv()
        c.fr.start()
        c.l1.wait_recv()
        c.fl.start()

    def forward_near(pt):
        c = spin[pt]
        c.r1.wait_recv()
        c.sl.start()
        c.l0.wait_recv()
        c.sr.start()

    def end_ring(pt):
        c = spin[pt]
        c.fr.wait_recv()
        c.s0.start()
        c.fl.wait_recv()
        c.s1.start()

    def up_tile(pt, p, n):
        cols = pl.ds(pl.multiple_of(n * 512, 512), 512)
        a = pl.ds(pl.multiple_of((p % 2) * HIDDEN, HIDDEN), QUARTER)
        b = pl.ds(pl.multiple_of((p % 2) * HIDDEN + QUARTER, QUARTER), QUARTER)
        rows = slice(pt * HALF, (pt + 1) * HALF)
        return dot(x[2 * p, rows], r.upv[a, cols]) + dot(x[2 * p + 1, rows], r.upv[b, cols]), cols

    def up_first(pt, p):
        def tile(n, carry):
            value, cols = up_tile(pt, p, n)
            r.pre[:, cols] = value
            return carry

        lax.fori_loop(0, 3, tile, 0)

    def up_second(pt, p, at):
        def tile(n, carry):
            value, cols = up_tile(pt, p, n)
            value = r.pre[:, cols] + value
            if pt == 0:
                value, slope = curves(value)
                r.slope[at, :, cols] = slope.astype(BF)
            else:
                value = value * r.slope[at, :, cols].astype(F32)
            r.act[pt, at, :, cols] = value.astype(BF)
            return carry

        lax.fori_loop(0, 3, tile, 0)

    dests = (off, right, left, pos)

    def out_ref(pt, i):
        return r.down_out.at[i] if pt == 0 else x.at[i, pl.ds(0, HALF)]

    def down_part(pt, i, core_to):
        p = dests[i]
        at = jnp.where(p // 2 == xh, 0, 1)
        cols = pl.ds(pl.multiple_of(((p % 2) * 2 + core_to) * QUARTER, QUARTER), QUARTER)
        out_ref(pt, 2 * i + (0 if core_to is not co else 1))[...] = dot(r.act[pt, at], r.downv[:, cols]).astype(BF)

    def add(pt, i, h, *more):
        dst = out_ref(pt, 2 * i + 1)
        cols = slice(h * COLS, (h + 1) * COLS)

        def step(n, carry):
            at = pl.ds(pl.multiple_of(n * 80, 80), 80)
            value = dst[at, cols].astype(F32) + r.sibin[pt, i, at, cols].astype(F32)
            for ref in more:
                value = value + ref[pt, at].astype(F32)
            dst[at, cols] = value.astype(BF)
            return carry

        lax.fori_loop(0, HALF // 80, step, 0)

    def sum_copies(pt):
        def move(n, src, dst, peer):
            return remote(src, dst, r.r_s.at[pt * 10 + n], r.r_r.at[pt * 10 + n], peer)

        def piece(i, h):
            return out_ref(pt, 2 * i + 1).at[:, half_cols(h)]

        return types.SimpleNamespace(
            sib=[move(i, out_ref(pt, 2 * i), r.sibin.at[pt, i], to_sib) for i in range(4)],
            off_r=move(4, piece(0, 0), r.fwd_l.at[pt], to_r),
            off_l=move(5, piece(0, 1), r.fwd_r.at[pt], to_l),
            r0=move(6, piece(1, 0), r.fin_l.at[pt, :, half_cols(0)], to_r),
            r1=move(7, piece(1, 1), r.fin_l.at[pt, :, half_cols(1)], to_r),
            l0=move(8, piece(2, 0), r.fin_r.at[pt, :, half_cols(0)], to_l),
            l1=move(9, piece(2, 1), r.fin_r.at[pt, :, half_cols(1)], to_l),
        )

    sums = [sum_copies(pt) for pt in range(2)]

    def both_parts(pt, i):
        down_part(pt, i, 1 - co)
        sums[pt].sib[i].start()
        down_part(pt, i, co)

    def start_sums(pt):
        c = sums[pt]
        c.sib[0].wait_recv()
        add(pt, 0, 0)
        c.off_r.start()
        add(pt, 0, 1)
        c.off_l.start()

    def neighbour_sums(pt):
        c = sums[pt]
        c.sib[1].wait_recv()
        add(pt, 1, 1)
        c.r1.start()
        c.sib[2].wait_recv()
        add(pt, 2, 0)
        c.l0.start()

    def forward_sums(pt):
        c = sums[pt]
        c.off_r.wait_recv()
        add(pt, 1, 0, r.fwd_l)
        c.r0.start()
        c.off_l.wait_recv()
        add(pt, 2, 1, r.fwd_r)
        c.l1.start()

    def leave(pt):
        c = sums[pt]
        for copy in (c.sib[3], c.r1, c.l0, c.r0, c.l1):
            copy.wait_recv()
        own = out_ref(pt, 7)

        def step(g, carry):
            at = pl.ds(pl.multiple_of(g * GROUP, GROUP), GROUP)
            value = (own[at].astype(F32) + r.sibin[pt, 3, at].astype(F32)) + (
                r.fin_l[pt, at].astype(F32) + r.fin_r[pt, at].astype(F32)
            )
            r.total[pt, at] = value.astype(BF)
            return carry

        lax.fori_loop(0, 4, step, 0)
        moves = plane(
            pt, 0, lambda s: r.total.at[pt, rows_of(s)], lambda s: r.bmain.at[pt, s], r.b_s, r.b_r, 19
        )
        rest = jnp.concatenate([r.total[pt, i * GROUP + 64 : (i + 1) * GROUP] for i in range(4)], axis=0)
        value = jnp.zeros((256, 256), F32)
        for g in range(3):
            value = value + dot(piece_rows(g), rest[:, g * 256 : (g + 1) * 256], TN)
        r.trest[pt] = value.astype(BF).reshape(EXPERTS, MAIN, 256)
        return moves + plane(
            pt, 1, lambda s: r.trest.at[pt, s], lambda s: r.brest.at[pt, s], r.b_s, r.b_r, 19
        )

    merge(0)
    start_projection(0)
    end_projection(0)
    moves = start_mean(0)
    gain = 1.0 + r.scalev[...]
    recip = lax.rsqrt(end_mean(0, moves) + EPS)
    sf = r.state[0].astype(F32)
    r.normed[0] = (sf * recip * gain + r.shiftv[...]).astype(BF)
    route0 = route(0)

    for a, b in YX:
        out_copies(a, b, 1)[0].wait()
    merge(1)
    start_projection(1)
    end_route(0, route0)
    start_ring(0)
    end_projection(1)
    moves = start_mean(1)
    cross = end_mean(1, moves)
    sf, tf = r.state[0].astype(F32), r.state[1].astype(F32)
    r.normed[1] = ((tf * recip - sf * (recip * recip * recip) * cross) * gain).astype(BF)
    route1 = route(1)
    both = r.normed[...].reshape(2 * TOK, QUARTER)
    r.mlog[...] = dot(r.routerv[...], both, NT)
    log_moves = [
        remote(r.mlog, r.glog.at[n], r.g_s.at[n], r.g_r.at[n], peer) for n, peer in enumerate(peers_e)
    ]
    for copy in log_moves:
        copy.start()

    for copy in local[13:]:
        copy.wait()
    c0, c1 = spin
    c0.own.wait_recv()
    up_first(0, pos)
    forward_far(0)
    forward_near(0)
    end_route(1, route1)
    start_ring(1)
    c0.sl.wait_recv()
    c0.sr.wait_recv()
    up_second(0, pair, 0)
    end_ring(0)
    up_first(0, other)
    c0.s0.wait_recv()
    c0.s1.wait_recv()
    up_second(0, off, 1)
    both_parts(0, 0)
    forward_far(1)
    start_sums(0)
    forward_near(1)
    c1.own.wait_recv()
    up_first(1, pos)
    both_parts(0, 1)
    c1.sl.wait_recv()
    c1.sr.wait_recv()
    up_second(1, pair, 0)
    end_ring(1)
    both_parts(0, 2)
    neighbour_sums(0)
    forward_sums(0)
    up_first(1, other)
    c1.s0.wait_recv()
    c1.s1.wait_recv()
    up_second(1, off, 1)
    for c in spin:
        for copy in vars(c).values():
            copy.wait_send()
    both_parts(1, 0)
    both_parts(0, 3)
    start_sums(1)
    both_parts(1, 1)
    both_parts(1, 2)
    neighbour_sums(1)
    back0 = leave(0)
    forward_sums(1)
    both_parts(1, 3)

    for copy in log_moves:
        copy.wait()
    logits = (r.mlog[...] + r.glog[0]) + (r.glog[1] + r.glog[2])
    ll, lt = logits[:, :TOK], logits[:, TOK:]
    own0 = jnp.sum(oh0 * ll, axis=0, keepdims=True)
    own1 = jnp.sum(oh1 * ll, axis=0, keepdims=True)
    diff = jnp.sum(oh0 * lt, axis=0, keepdims=True) - jnp.sum(oh1 * lt, axis=0, keepdims=True)
    gate0 = 1.0 / (1.0 + jnp.exp(own1 - own0))
    gate1 = 1.0 / (1.0 + jnp.exp(own0 - own1))
    gates = oh0 * gate0 + oh1 * gate1
    gates_tan = oh0 * (gate0 * (1.0 - gate0) * diff) - oh1 * (gate1 * (1.0 - gate1) * diff)
    main = r.sel[0].astype(F32)
    rest = (r.sel[1] + r.sel[2] + r.sel[3]).astype(F32)
    for i, g in enumerate((gates, gates_tan)):
        high = g.astype(BF)
        low = (g - high.astype(F32)).astype(BF)
        at = slice(i * TOK, (i + 1) * TOK)
        for j, item in enumerate((high, low)):
            wide = dot(item, spread, TN)
            r.gates[j, at] = (main * wide).astype(BF)
            r.gates[2 + j, at] = (rest * wide).astype(BF)

    back1 = leave(1)
    for c in sums:
        for copy in c.sib + [c.off_r, c.off_l, c.r0, c.r1, c.l0, c.l1]:
            copy.wait_send()

    def gated(pt, lhs):
        out = []
        for g in range(3):
            value = jnp.zeros((lhs.stop - lhs.start, 256), F32)
            rows = r.bmain[pt, :, :, g * 256 : (g + 1) * 256].reshape(256, 256)
            rest = r.brest[pt].reshape(256, 256)
            mask = iota((lhs.stop - lhs.start, 256), 1) % MAIN // 4 == g
            for j in range(2):
                value = value + dot(r.gates[j, lhs], rows)
                value = value + dot(jnp.where(mask, r.gates[2 + j, lhs], jnp.zeros((), BF)), rest)
            out.append(value)
        return out

    for copy in back0:
        copy.wait()
    primal = gated(0, slice(0, 2 * TOK))
    for g in range(3):
        at = slice(g * 256, (g + 1) * 256)
        r.mixed[:, at] = (r.state[0, :, at].astype(F32) + primal[g][:TOK]).astype(BF)
        r.kept[:, at] = r.state[1, :, at].astype(F32) + primal[g][TOK:]
    for copy in back1:
        copy.wait()
    tangent = gated(1, slice(0, TOK))
    for g in range(3):
        at = slice(g * 256, (g + 1) * 256)
        r.mixed_tan[:, at] = (r.kept[:, at] + tangent[g]).astype(BF)


def shards(
    residual_in, residual_tan, queries, keys, values, query_tan, key_tan, value_tan,
    out_proj, shift_mod, scale_mod, router, up_weight, down_weight, expert_ids,
):
    out = jax.ShapeDtypeStruct((TOK, QUARTER), BF)
    return pl.pallas_call(
        block_kernel,
        out_shape=(out, out),
        in_specs=[pl.BlockSpec(memory_space=pl.ANY)] * 15,
        out_specs=(pl.BlockSpec(memory_space=VMEM),) * 2,
        scratch_shapes=list(SCRATCH.values()),
        compiler_params=pltpu.CompilerParams(
            collective_id=1, has_side_effects=True, vmem_limit_bytes=64 * MIB - 64 * 1024
        ),
        name="block",
    )(
        queries, query_tan, keys, values, key_tan, value_tan, out_proj, residual_in, residual_tan,
        up_weight, down_weight, router.T, shift_mod[None], scale_mod[None], expert_ids.T,
    )


def solution(mesh):
    rows, heads = P("ctx", "exp"), P("exp", None)
    in_specs = (rows,) * 8 + (
        heads, P(), P(), P(), P("ctx", None, "exp"), P("ctx", "exp", None), P("ctx", None),
    )
    return jax.shard_map(shards, mesh=mesh, in_specs=in_specs, out_specs=(rows, rows), check_vma=False)
```

```python
import functools
import types

import jax
import jax.numpy as jnp
from jax import lax
from jax.experimental import pallas as pl
from jax.experimental.pallas import tpu as pltpu
from jax.sharding import PartitionSpec as P

D = 3072
HD = 128
TOK = 128
HEADS_HERE = 3
WIDTH = HEADS_HERE * HD
QUARTER = 768
EXPERTS = 16
CAP = 20
MAIN = 16
GROUP = 4 * CAP
ROWS = 640
HALF = ROWS // 2
COLS = QUARTER // 2
HIDDEN = 1536
EPS = 1e-06
FACTOR = HD ** (-0.5)
LOG2E = 1.4426950408889634
MIB = 2**20

BF = jnp.bfloat16
F32 = jnp.float32
MESH = pl.DeviceIdType.MESH
VMEM = pltpu.VMEM
NT = (((1,), (1,)), ((), ()))
TN = (((0,), (0,)), ((), ()))
NN = (((1,), (0,)), ((), ()))


def dot(a, b, dims=NN):
    return lax.dot_general(a, b, dims, preferred_element_type=F32)


def coords():
    c = lax.axis_index("ctx")
    e = lax.axis_index("exp")
    return c // 8, (c // 2) % 4, c % 2, e // 2, e % 2


def device(z, y, xh, xl, core):
    return (z * 8 + y * 2 + xh, xl * 2 + core)


def meet(peers):
    barrier = pltpu.get_barrier_semaphore()
    for peer in peers:
        pl.semaphore_signal(barrier, inc=1, device_id=peer, device_id_type=MESH)
    pl.semaphore_wait(barrier, len(peers))


def remote(src, dst, send, recv, peer):
    return pltpu.make_async_remote_copy(
        src_ref=src, dst_ref=dst, send_sem=send, recv_sem=recv, device_id=peer, device_id_type=MESH
    )


YX = [(0, 1)] + [(a, b) for a in (1, 3, 2) for b in (0, 1)]
ZY = [(a, b) for a in (2, 1, 3, 0) for b in (2, 1, 3, 0) if a or b]

INPUTS = (
    "q", "qt", "k", "v", "kt", "vt", "out_proj", "res", "rest", "up", "down", "router",
    "shift", "scale", "ids",
)
OUTPUTS = ("mixed", "mixed_tan")


def sems(n):
    return pltpu.SemaphoreType.DMA((n,))


SCRATCH = {
    "qg": VMEM((8, TOK, WIDTH), BF),
    "qtg": VMEM((8, TOK, WIDTH), BF),
    "kg": VMEM((4, TOK, WIDTH), BF),
    "ktg": VMEM((4, TOK, WIDTH), BF),
    "vg": VMEM((4, TOK, WIDTH), BF),
    "vtg": VMEM((4, TOK, WIDTH), BF),
    "ot": VMEM((2, 8, TOK, WIDTH), BF),
    "got": VMEM((2, 8, TOK, WIDTH), BF),
    "stats": VMEM((8, 8, TOK), F32),
    "gstats": VMEM((8, 8, TOK), F32),
    "proj": VMEM((WIDTH, D), BF),
    "state": VMEM((2, TOK, QUARTER), BF),
    "routerv": VMEM((EXPERTS, QUARTER), BF),
    "shiftv": VMEM((1, QUARTER), F32),
    "scalev": VMEM((1, QUARTER), F32),
    "idsv": VMEM((2, TOK), jnp.int32),
    "mine": VMEM((2, 2, TOK, QUARTER), BF),
    "sib": VMEM((2, 2, TOK, QUARTER), BF),
    "far": VMEM((2, TOK, QUARTER), BF),
    "farin": VMEM((2, TOK, QUARTER), BF),
    "mstat": VMEM((2, 8, TOK), F32),
    "gstat": VMEM((2, 3, 8, TOK), F32),
    "mlog": VMEM((EXPERTS, 2 * TOK), F32),
    "glog": VMEM((3, EXPERTS, 2 * TOK), F32),
    "acc": VMEM((2, TOK, WIDTH), BF),
    "kept": VMEM((TOK, QUARTER), F32),
    "normed": VMEM((2, TOK, QUARTER), BF),
    "gates": VMEM((4, 2 * TOK, 256), BF),
    "sel": VMEM((4, TOK, 256), BF),
    "pmain": VMEM((2, EXPERTS, MAIN, QUARTER), BF),
    "prest": VMEM((2, EXPERTS, MAIN, 256), BF),
    "zrest": VMEM((2, EXPERTS, MAIN, 256), BF),
    "upv": VMEM((D, HIDDEN), BF),
    "downv": VMEM((HIDDEN, D), BF),
    "x": VMEM((8, ROWS, QUARTER), BF),
    "pre": VMEM((HALF, HIDDEN), F32),
    "slope": VMEM((2, HALF, HIDDEN), BF),
    "act": VMEM((2, 2, HALF, HIDDEN), BF),
    "down_out": VMEM((8, HALF, QUARTER), BF),
    "sibin": VMEM((2, 4, HALF, QUARTER), BF),
    "fwd_l": VMEM((2, HALF, COLS), BF),
    "fwd_r": VMEM((2, HALF, COLS), BF),
    "fin_l": VMEM((2, HALF, QUARTER), BF),
    "fin_r": VMEM((2, HALF, QUARTER), BF),
    "total": VMEM((2, HALF, QUARTER), BF),
    "trest": VMEM((2, EXPERTS, MAIN, 256), BF),
    "bmain": VMEM((2, EXPERTS, MAIN, QUARTER), BF),
    "brest": VMEM((2, EXPERTS, MAIN, 256), BF),
    "lsem": sems(27),
    "kv_s": sems(12), "kv_r": sems(12),
    "q_s": sems(16), "q_r": sems(16),
    "o_s": sems(24), "o_r": sems(24),
    "p_s": sems(6), "p_r": sems(6),
    "t_s": sems(6), "t_r": sems(6),
    "g_s": sems(3), "g_r": sems(3),
    "z_s": sems(60), "z_r": sems(60),
    "a_s": sems(22), "a_r": sems(22),
    "r_s": sems(20), "r_r": sems(20),
    "b_s": sems(60), "b_r": sems(60),
}


def to_columns(rows):
    n = rows.shape[0]
    return jnp.concatenate([rows, jnp.zeros((128 - n, 128), F32)], axis=0).T


def attend(r, yp):
    at = pl.ds(2 * yp, 2)
    for h in range(HEADS_HERE):
        c = slice(h * HD, (h + 1) * HD)
        qh, qth = r.qg[at, :, c].reshape(256, HD), r.qtg[at, :, c].reshape(256, HD)
        kh, kth = r.kg[:, :, c].reshape(512, HD), r.ktg[:, :, c].reshape(512, HD)
        vh, vth = r.vg[:, :, c].reshape(512, HD), r.vtg[:, :, c].reshape(512, HD)
        scores = dot(kh, qh, NT) * (FACTOR * LOG2E)
        tan = dot(jnp.concatenate([kh, kth], 1), jnp.concatenate([qth, qh], 1), NT) * FACTOR
        high = jnp.max(scores, axis=0, keepdims=True)
        weights = jnp.exp2(scores - high)
        total = jnp.sum(weights, axis=0, keepdims=True)
        weights = weights * (1.0 / total)
        mean = jnp.sum(weights * tan, axis=0, keepdims=True)
        tilted = (weights * (tan - mean)).astype(BF)
        both = dot(weights.astype(BF), jnp.concatenate([vh, vth], 1), TN)
        tout = both[:, HD:] + dot(tilted, vh, TN)
        r.ot[0, at, :, c] = both[:, :HD].astype(BF).reshape(2, TOK, HD)
        r.ot[1, at, :, c] = tout.astype(BF).reshape(2, TOK, HD)
        lse = high + jnp.log2(total)
        for i in range(2):
            part = slice(i * TOK, (i + 1) * TOK)
            r.stats[2 * yp + i, h : h + 1, :] = lse[:, part]
            r.stats[2 * yp + i, 4 + h : 5 + h, :] = mean[:, part]


def curves(x):
    sq = x * x
    th = jnp.tanh(0.7978845608028654 * x * (1.0 + 0.044715 * sq))
    half = 0.5 * (1.0 + th)
    slope = half + 0.5 * x * (1.0 - th * th) * (0.7978845608028654 * (1.0 + 0.134145 * sq))
    return x * half, slope


def block_kernel(*refs):
    r = types.SimpleNamespace(**dict(zip(INPUTS + OUTPUTS + tuple(SCRATCH), refs)))
    z, y, xh, xl, co = coords()
    e = xl * 2 + co
    pos = xh * 2 + xl
    here_q = y * 2 + xh
    here = z * 4 + y
    right, left, off = (pos + 1) % 4, (pos + 3) % 4, (pos + 2) % 4
    pair, other = xh * 2 + 1 - xl, (1 - xh) * 2 + 1 - xl

    def at_pos(p, c):
        return device(z, y, p // 2, p % 2, c)

    def near(a, b):
        return device(z, (y + a) % 4, (xh + b) % 2, xl, co)

    to_r, to_l, to_sib = at_pos(right, co), at_pos(left, co), at_pos(pos, 1 - co)
    across, diagonal = at_pos(pair, co), at_pos(pair, 1 - co)
    peers_e = [to_sib, across, diagonal]
    peers_zy = [device((z + a) % 4, (y + b) % 4, xh, xl, co) for a, b in ZY]
    meet(peers_zy + [near(a, 1) for a in range(4)] + peers_e + [at_pos(other, co)])

    z_up, z_down = device((z + 1) % 4, y, xh, xl, co), device((z + 3) % 4, y, xh, xl, co)
    y_up, y_down = near(1, 0), near(3, 0)

    def kv_copy(n, src, dst, at, peer):
        return remote(src, dst.at[at], r.kv_s.at[n], r.kv_r.at[n], peer)

    kv_pairs = ((r.k, r.kg), (r.kt, r.ktg), (r.v, r.vg), (r.vt, r.vtg))
    kv_up = [kv_copy(i, src, dst, z, z_up) for i, (src, dst) in enumerate(kv_pairs)]
    kv_down = [kv_copy(4 + i, src, dst, z, z_down) for i, (src, dst) in enumerate(kv_pairs)]
    z_before, z_after = (z + 3) % 4, (z + 1) % 4
    kv_on = [
        kv_copy(8, r.kg.at[z_before], r.kg, z_before, z_up),
        kv_copy(9, r.ktg.at[z_before], r.ktg, z_before, z_up),
        kv_copy(10, r.vg.at[z_after], r.vg, z_after, z_down),
        kv_copy(11, r.vtg.at[z_after], r.vtg, z_after, z_down),
    ]

    def q_copy(n, src, dst, at, peer):
        return remote(src, dst.at[at], r.q_s.at[n], r.q_r.at[n], peer)

    q_pairs = ((r.q, r.qg), (r.qt, r.qtg))
    q_over = [q_copy(i, src, dst, here_q, near(0, 1)) for i, (src, dst) in enumerate(q_pairs)]
    there_q = y * 2 + 1 - xh

    def q_round(n, sources, side):
        mine = y * 2 + side
        low, high = ((y + 3) % 4) * 2 + side, ((y + 1) % 4) * 2 + side
        up = [q_copy(n + i, src, dst, mine, y_up) for i, (src, dst) in enumerate(zip(sources, (r.qg, r.qtg)))]
        down = [q_copy(n + 2 + i, src, dst, mine, y_down) for i, (src, dst) in enumerate(zip(sources, (r.qg, r.qtg)))]
        on = [
            q_copy(n + 4, r.qg.at[low], r.qg, low, y_up),
            q_copy(n + 5, r.qtg.at[high], r.qtg, high, y_down),
        ]
        return up, down, on

    q_own = q_round(2, (r.q, r.qt), xh)
    q_other = q_round(8, (r.qg.at[there_q], r.qtg.at[there_q]), 1 - xh)

    def start_round(group):
        up, down, on = group
        for copy in (up[0], down[1], up[1], down[0]):
            copy.start()

    def pass_round(group):
        up, down, on = group
        up[0].wait_recv()
        on[0].start()
        down[1].wait_recv()
        on[1].start()

    for n in (0, 1):
        q_over[n].start()
        kv_up[n].start()
        kv_down[2 + n].start()
    start_round(q_own)
    for n in (0, 1):
        kv_up[2 + n].start()
        kv_down[n].start()
    kv = kv_up + kv_down + kv_on
    queries = q_over + [copy for group in q_own + q_other for copy in group]
    quarter = pl.ds(pl.multiple_of(e * QUARTER, QUARTER), QUARTER)
    local = [
        pltpu.make_async_copy(src, dst, r.lsem.at[i])
        for i, (src, dst) in enumerate(
            (
                (r.k, r.kg.at[z]), (r.kt, r.ktg.at[z]), (r.v, r.vg.at[z]), (r.vt, r.vtg.at[z]),
                (r.q, r.qg.at[here_q]), (r.qt, r.qtg.at[here_q]),
                (r.out_proj, r.proj), (r.res, r.state.at[0]), (r.rest, r.state.at[1]),
                (r.router.at[:, quarter], r.routerv),
                (r.shift.at[:, quarter], r.shiftv), (r.scale.at[:, quarter], r.scalev), (r.ids, r.idsv),
                (r.up.at[0], r.upv), (r.down.at[0], r.downv),
            )
        )
    ]
    for copy in local:
        copy.start()

    r.stats[...] = jnp.zeros_like(r.stats)
    local[12].wait()
    expert = lax.broadcasted_iota(jnp.int32, (EXPERTS, TOK), 0)
    oh0 = (r.idsv[0:1, :] == expert).astype(F32)
    oh1 = (r.idsv[1:2, :] == expert).astype(F32)
    named = (oh0 + oh1).astype(BF)

    def iota(shape, dim):
        return lax.broadcasted_iota(jnp.int32, shape, dim)

    before = (iota((TOK, TOK), 0) < iota((TOK, TOK), 1)).astype(BF)
    rank = dot(named, before).astype(BF)
    spread = (iota((EXPERTS, 256), 1) // MAIN == iota((EXPERTS, 256), 0)).astype(BF)

    named_x = dot(named, spread, TN)
    rank_x = dot(rank, spread, TN)
    slot = iota((TOK, 256), 1) % MAIN
    r.sel[0] = jnp.where(rank_x == slot.astype(F32), named_x, 0.0).astype(BF)
    extra = jnp.where(rank_x == (MAIN + slot % 4).astype(F32), named_x, 0.0)
    for g in range(3):
        r.sel[1 + g] = jnp.where(slot // 4 == g, extra, 0.0).astype(BF)

    def out_copies(a, b, part):
        n = 6 * a + 3 * b
        there = ((y + a) % 4) * 2 + (xh + b) % 2
        moves = [
            remote(
                r.ot.at[part, there], r.got.at[part, here_q], r.o_s.at[n + part], r.o_r.at[n + part], near(a, b)
            )
        ]
        if part == 0:
            moves.append(
                remote(r.stats.at[there], r.gstats.at[here_q], r.o_s.at[n + 2], r.o_r.at[n + 2], near(a, b))
            )
        return moves

    for copy in q_over:
        copy.wait_recv()
    start_round(q_other)
    for n in (0, 1):
        kv_up[n].wait_recv()
        kv_on[n].start()
        kv_down[2 + n].wait_recv()
        kv_on[2 + n].start()
    pass_round(q_own)
    pass_round(q_other)
    for copy in local[:6]:
        copy.wait()
    for copy in kv_up[2:] + kv_down[:2] + kv_on:
        copy.wait_recv()
    for up, down, on in (q_own, q_other):
        for copy in (up[1], down[0], on[0], on[1]):
            copy.wait_recv()
    attend(r, y)
    for copy in out_copies(0, 1, 0):
        copy.start()
    keep = [
        pltpu.make_async_copy(r.stats.at[here_q], r.gstats.at[here_q], r.lsem.at[23]),
        pltpu.make_async_copy(r.ot.at[0, here_q], r.got.at[0, here_q], r.lsem.at[24]),
        pltpu.make_async_copy(r.ot.at[1, here_q], r.got.at[1, here_q], r.lsem.at[25]),
    ]
    for copy in keep:
        copy.start()

    def attend_step(i, carry):
        a = 1 + 2 * i - 3 * (i // 2)
        attend(r, (y + 4 - a) % 4)
        for b in (0, 1):
            for copy in out_copies(4 - a, b, 0):
                copy.start()
        return carry

    lax.fori_loop(0, 3, attend_step, 0)
    for a, b in YX:
        out_copies(a, b, 1)[0].start()
    for copy in kv:
        copy.wait_send()
    for copy in queries:
        copy.wait_send()
    for copy in local[6:12] + keep:
        copy.wait()
    for a, b in YX:
        for copy in out_copies(a, b, 0):
            copy.wait()

    lse = [r.gstats[j, 0:3, :] for j in range(8)]
    mean = [r.gstats[j, 4:7, :] for j in range(8)]
    top = functools.reduce(jnp.maximum, lse)
    part = [jnp.exp2(item - top) for item in lse]
    inv = 1.0 / functools.reduce(jnp.add, part)
    part = [item * inv for item in part]
    mid = functools.reduce(jnp.add, [p * m for p, m in zip(part, mean)])
    lean = [p * (m - mid) for p, m in zip(part, mean)]
    cols = to_columns(jnp.concatenate(part + lean, axis=0))

    def merge(pt):
        for h in range(HEADS_HERE):
            at = slice(h * HD, (h + 1) * HD)
            sum_ = jnp.zeros((TOK, HD), F32)
            for j in range(8):
                w = cols[:, j * 3 + h : j * 3 + h + 1]
                sum_ = sum_ + w * r.got[pt, j, :, at].astype(F32)
                if pt == 1:
                    c = cols[:, 24 + j * 3 + h : 24 + j * 3 + h + 1]
                    sum_ = sum_ + c * r.got[0, j, :, at].astype(F32)
            r.acc[pt, :, at] = sum_.astype(BF)

    def project(pt, xl_to, core_to):
        at = pl.multiple_of((xl_to * 2 + core_to) * QUARTER, QUARTER)
        return dot(r.acc[pt], r.proj[:, pl.ds(at, QUARTER)])

    def project_move(pt, n, src, dst, peer):
        return remote(src, dst, r.p_s.at[pt * 3 + n], r.p_r.at[pt * 3 + n], peer)

    to_sib0 = [project_move(pt, 0, r.mine.at[pt, 0], r.sib.at[pt, 0], to_sib) for pt in range(2)]
    to_sib1 = [project_move(pt, 1, r.mine.at[pt, 1], r.sib.at[pt, 1], to_sib) for pt in range(2)]
    to_far = [project_move(pt, 2, r.far.at[pt], r.farin.at[pt], across) for pt in range(2)]

    def start_projection(pt):
        r.mine[pt, 0] = project(pt, 1 - xl, 1 - co).astype(BF)
        to_sib0[pt].start()
        r.mine[pt, 1] = project(pt, xl, 1 - co).astype(BF)
        to_sib1[pt].start()
        away = project(pt, 1 - xl, co)
        to_sib0[pt].wait()
        r.far[pt] = (away + r.sib[pt, 0].astype(F32)).astype(BF)
        to_far[pt].start()
        kept = project(pt, xl, co)
        to_sib1[pt].wait()
        r.kept[...] = kept + r.sib[pt, 1].astype(F32) + r.state[pt].astype(F32)

    def end_projection(pt):
        to_far[pt].wait()
        r.state[pt] = (r.kept[...] + r.farin[pt].astype(F32)).astype(BF)

    def start_mean(pt):
        product = jnp.sum(r.state[0].astype(F32) * r.state[pt].astype(F32), axis=1, keepdims=True)
        r.mstat[pt] = jnp.broadcast_to(product, (TOK, 128)).T[0:8]
        moves = [
            remote(r.mstat.at[pt], r.gstat.at[pt, n], r.t_s.at[pt * 3 + n], r.t_r.at[pt * 3 + n], peer)
            for n, peer in enumerate(peers_e)
        ]
        for copy in moves:
            copy.start()
        return moves

    def end_mean(pt, moves):
        for copy in moves:
            copy.wait()
        rows = (r.mstat[pt] + r.gstat[pt, 0]) + (r.gstat[pt, 1] + r.gstat[pt, 2])
        return to_columns(rows)[:, 0:1] * (1.0 / D)

    block = pos * 2 + co

    def rows_of(source):
        return pl.ds(pl.multiple_of((source // 4) * GROUP + (source % 4) * MAIN, MAIN), MAIN)

    def x_rows_of(pt, source):
        return pl.ds(pl.multiple_of(pt * HALF + (source // 4) * GROUP + (source % 4) * MAIN, MAIN), MAIN)

    def plane(pt, i, src, dst, send, recv, lsem):
        moves = []
        for n, ((a, b), peer) in enumerate(zip(ZY, peers_zy)):
            there = ((z + a) % 4) * 4 + (y + b) % 4
            at = pt * 30 + i * 15 + n
            moves.append(remote(src(there), dst(here), send.at[at], recv.at[at], peer))
        moves.append(pltpu.make_async_copy(src(here), dst(here), r.lsem.at[lsem + 2 * pt + i]))
        for copy in moves:
            copy.start()
        return moves

    def route(pt):
        rows = r.normed[pt]
        r.pmain[pt] = dot(r.sel[0], rows, TN).astype(BF).reshape(EXPERTS, MAIN, QUARTER)
        moves = plane(
            pt, 0, lambda s: r.pmain.at[pt, s], lambda s: r.x.at[block, x_rows_of(pt, s)], r.z_s, r.z_r, 15
        )
        value = jnp.zeros((256, 256), F32)
        for g in range(3):
            value = value + dot(r.sel[1 + g], rows[:, g * 256 : (g + 1) * 256], TN)
        r.prest[pt] = value.astype(BF).reshape(EXPERTS, MAIN, 256)
        return moves + plane(
            pt, 1, lambda s: r.prest.at[pt, s], lambda s: r.zrest.at[pt, s], r.z_s, r.z_r, 15
        )

    def piece_rows(g):
        to, source = iota((64, 256), 0), iota((64, 256), 1)
        return ((to // 4 == source // MAIN) & (source % MAIN == 4 * g + to % 4)).astype(BF)

    def end_route(pt, moves):
        for copy in moves:
            copy.wait()
        rest = r.zrest[pt].reshape(256, 256)
        for g in range(3):
            value = dot(piece_rows(g), rest).astype(BF)
            for i in range(4):
                at = slice(pt * HALF + i * GROUP + 64, pt * HALF + (i + 1) * GROUP)
                r.x[block, at, g * 256 : (g + 1) * 256] = value[i * 16 : (i + 1) * 16]

    x = r.x
    bl, br, bo = left * 2 + co, right * 2 + co, off * 2 + co

    def half_cols(h):
        return pl.ds(h * COLS, COLS)

    def pass_on(pt, n, b, h, peer):
        cols = pl.ds(0, QUARTER) if h is None else half_cols(h)
        ref = x.at[b, pl.ds(pt * HALF, HALF), cols]
        return remote(ref, ref, r.a_s.at[pt * 11 + n], r.a_r.at[pt * 11 + n], peer)

    def ring_copies(pt):
        return types.SimpleNamespace(
            own=pass_on(pt, 0, block, None, to_sib),
            r0=pass_on(pt, 1, block, 0, to_r),
            r1=pass_on(pt, 2, block, 1, to_r),
            l1=pass_on(pt, 3, block, 1, to_l),
            l0=pass_on(pt, 4, block, 0, to_l),
            fr=pass_on(pt, 5, bl, 0, to_r),
            fl=pass_on(pt, 6, br, 1, to_l),
            sl=pass_on(pt, 7, bl, None, to_sib),
            sr=pass_on(pt, 8, br, None, to_sib),
            s0=pass_on(pt, 9, bo, 0, to_sib),
            s1=pass_on(pt, 10, bo, 1, to_sib),
        )

    spin = [ring_copies(pt) for pt in range(2)]

    def start_ring(pt):
        c = spin[pt]
        for copy in (c.r0, c.l1, c.r1, c.l0, c.own):
            copy.start()

    def forward_far(pt):
        c = spin[pt]
        c.r0.wait_recv()
        c.fr.start()
        c.l1.wait_recv()
        c.fl.start()

    def forward_near(pt):
        c = spin[pt]
        c.r1.wait_recv()
        c.sl.start()
        c.l0.wait_recv()
        c.sr.start()

    def end_ring(pt):
        c = spin[pt]
        c.fr.wait_recv()
        c.s0.start()
        c.fl.wait_recv()
        c.s1.start()

    def up_tile(pt, p, n):
        cols = pl.ds(pl.multiple_of(n * 512, 512), 512)
        a = pl.ds(pl.multiple_of((p % 2) * HIDDEN, HIDDEN), QUARTER)
        b = pl.ds(pl.multiple_of((p % 2) * HIDDEN + QUARTER, QUARTER), QUARTER)
        rows = slice(pt * HALF, (pt + 1) * HALF)
        return dot(x[2 * p, rows], r.upv[a, cols]) + dot(x[2 * p + 1, rows], r.upv[b, cols]), cols

    def up_first(pt, p):
        def tile(n, carry):
            value, cols = up_tile(pt, p, n)
            r.pre[:, cols] = value
            return carry

        lax.fori_loop(0, 3, tile, 0)

    def up_second(pt, p, at):
        def tile(n, carry):
            value, cols = up_tile(pt, p, n)
            value = r.pre[:, cols] + value
            if pt == 0:
                value, slope = curves(value)
                r.slope[at, :, cols] = slope.astype(BF)
            else:
                value = value * r.slope[at, :, cols].astype(F32)
            r.act[pt, at, :, cols] = value.astype(BF)
            return carry

        lax.fori_loop(0, 3, tile, 0)

    dests = (off, right, left, pos)

    def out_ref(pt, i):
        return r.down_out.at[i] if pt == 0 else x.at[i, pl.ds(0, HALF)]

    def down_part(pt, i, core_to):
        p = dests[i]
        at = jnp.where(p // 2 == xh, 0, 1)
        cols = pl.ds(pl.multiple_of(((p % 2) * 2 + core_to) * QUARTER, QUARTER), QUARTER)
        out_ref(pt, 2 * i + (0 if core_to is not co else 1))[...] = dot(r.act[pt, at], r.downv[:, cols]).astype(BF)

    def add(pt, i, h, *more):
        dst = out_ref(pt, 2 * i + 1)
        cols = slice(h * COLS, (h + 1) * COLS)

        def step(n, carry):
            at = pl.ds(pl.multiple_of(n * 80, 80), 80)
            value = dst[at, cols].astype(F32) + r.sibin[pt, i, at, cols].astype(F32)
            for ref in more:
                value = value + ref[pt, at].astype(F32)
            dst[at, cols] = value.astype(BF)
            return carry

        lax.fori_loop(0, HALF // 80, step, 0)

    def sum_copies(pt):
        def move(n, src, dst, peer):
            return remote(src, dst, r.r_s.at[pt * 10 + n], r.r_r.at[pt * 10 + n], peer)

        def piece(i, h):
            return out_ref(pt, 2 * i + 1).at[:, half_cols(h)]

        return types.SimpleNamespace(
            sib=[move(i, out_ref(pt, 2 * i), r.sibin.at[pt, i], to_sib) for i in range(4)],
            off_r=move(4, piece(0, 0), r.fwd_l.at[pt], to_r),
            off_l=move(5, piece(0, 1), r.fwd_r.at[pt], to_l),
            r0=move(6, piece(1, 0), r.fin_l.at[pt, :, half_cols(0)], to_r),
            r1=move(7, piece(1, 1), r.fin_l.at[pt, :, half_cols(1)], to_r),
            l0=move(8, piece(2, 0), r.fin_r.at[pt, :, half_cols(0)], to_l),
            l1=move(9, piece(2, 1), r.fin_r.at[pt, :, half_cols(1)], to_l),
        )

    sums = [sum_copies(pt) for pt in range(2)]

    def both_parts(pt, i):
        down_part(pt, i, 1 - co)
        sums[pt].sib[i].start()
        down_part(pt, i, co)

    def start_sums(pt):
        c = sums[pt]
        c.sib[0].wait_recv()
        add(pt, 0, 0)
        c.off_r.start()
        add(pt, 0, 1)
        c.off_l.start()

    def neighbour_sums(pt):
        c = sums[pt]
        c.sib[1].wait_recv()
        add(pt, 1, 1)
        c.r1.start()
        c.sib[2].wait_recv()
        add(pt, 2, 0)
        c.l0.start()

    def forward_sums(pt):
        c = sums[pt]
        c.off_r.wait_recv()
        add(pt, 1, 0, r.fwd_l)
        c.r0.start()
        c.off_l.wait_recv()
        add(pt, 2, 1, r.fwd_r)
        c.l1.start()

    def leave(pt):
        c = sums[pt]
        for copy in (c.sib[3], c.r1, c.l0, c.r0, c.l1):
            copy.wait_recv()
        own = out_ref(pt, 7)

        def step(g, carry):
            at = pl.ds(pl.multiple_of(g * GROUP, GROUP), GROUP)
            value = (own[at].astype(F32) + r.sibin[pt, 3, at].astype(F32)) + (
                r.fin_l[pt, at].astype(F32) + r.fin_r[pt, at].astype(F32)
            )
            r.total[pt, at] = value.astype(BF)
            return carry

        lax.fori_loop(0, 4, step, 0)
        moves = plane(
            pt, 0, lambda s: r.total.at[pt, rows_of(s)], lambda s: r.bmain.at[pt, s], r.b_s, r.b_r, 19
        )
        rest = jnp.concatenate([r.total[pt, i * GROUP + 64 : (i + 1) * GROUP] for i in range(4)], axis=0)
        value = jnp.zeros((256, 256), F32)
        for g in range(3):
            value = value + dot(piece_rows(g), rest[:, g * 256 : (g + 1) * 256], TN)
        r.trest[pt] = value.astype(BF).reshape(EXPERTS, MAIN, 256)
        return moves + plane(
            pt, 1, lambda s: r.trest.at[pt, s], lambda s: r.brest.at[pt, s], r.b_s, r.b_r, 19
        )

    merge(0)
    start_projection(0)
    end_projection(0)
    moves = start_mean(0)
    gain = 1.0 + r.scalev[...]
    recip = lax.rsqrt(end_mean(0, moves) + EPS)
    sf = r.state[0].astype(F32)
    r.normed[0] = (sf * recip * gain + r.shiftv[...]).astype(BF)
    route0 = route(0)

    for a, b in YX:
        out_copies(a, b, 1)[0].wait()
    merge(1)
    start_projection(1)
    end_projection(1)
    moves = start_mean(1)
    end_route(0, route0)
    start_ring(0)
    cross = end_mean(1, moves)
    sf, tf = r.state[0].astype(F32), r.state[1].astype(F32)
    r.normed[1] = ((tf * recip - sf * (recip * recip * recip) * cross) * gain).astype(BF)
    route1 = route(1)
    both = r.normed[...].reshape(2 * TOK, QUARTER)
    r.mlog[...] = dot(r.routerv[...], both, NT)
    log_moves = [
        remote(r.mlog, r.glog.at[n], r.g_s.at[n], r.g_r.at[n], peer) for n, peer in enumerate(peers_e)
    ]
    for copy in log_moves:
        copy.start()

    for copy in local[13:]:
        copy.wait()
    c0, c1 = spin
    c0.own.wait_recv()
    up_first(0, pos)
    forward_far(0)
    forward_near(0)
    end_route(1, route1)
    start_ring(1)
    c0.sl.wait_recv()
    c0.sr.wait_recv()
    up_second(0, pair, 0)
    end_ring(0)
    up_first(0, other)
    c0.s0.wait_recv()
    c0.s1.wait_recv()
    up_second(0, off, 1)
    both_parts(0, 0)
    forward_far(1)
    start_sums(0)
    forward_near(1)
    c1.own.wait_recv()
    up_first(1, pos)
    both_parts(0, 1)
    c1.sl.wait_recv()
    c1.sr.wait_recv()
    up_second(1, pair, 0)
    end_ring(1)
    both_parts(0, 2)
    neighbour_sums(0)
    forward_sums(0)
    up_first(1, other)
    c1.s0.wait_recv()
    c1.s1.wait_recv()
    up_second(1, off, 1)
    for c in spin:
        for copy in vars(c).values():
            copy.wait_send()
    both_parts(1, 0)
    both_parts(0, 3)
    start_sums(1)
    both_parts(1, 1)
    both_parts(1, 2)
    neighbour_sums(1)
    back0 = leave(0)
    forward_sums(1)
    both_parts(1, 3)

    for copy in log_moves:
        copy.wait()
    logits = (r.mlog[...] + r.glog[0]) + (r.glog[1] + r.glog[2])
    ll, lt = logits[:, :TOK], logits[:, TOK:]
    own0 = jnp.sum(oh0 * ll, axis=0, keepdims=True)
    own1 = jnp.sum(oh1 * ll, axis=0, keepdims=True)
    diff = jnp.sum(oh0 * lt, axis=0, keepdims=True) - jnp.sum(oh1 * lt, axis=0, keepdims=True)
    gate0 = 1.0 / (1.0 + jnp.exp(own1 - own0))
    gate1 = 1.0 / (1.0 + jnp.exp(own0 - own1))
    gates = oh0 * gate0 + oh1 * gate1
    gates_tan = oh0 * (gate0 * (1.0 - gate0) * diff) - oh1 * (gate1 * (1.0 - gate1) * diff)
    main = r.sel[0].astype(F32)
    rest = (r.sel[1] + r.sel[2] + r.sel[3]).astype(F32)
    for i, g in enumerate((gates, gates_tan)):
        high = g.astype(BF)
        low = (g - high.astype(F32)).astype(BF)
        at = slice(i * TOK, (i + 1) * TOK)
        for j, item in enumerate((high, low)):
            wide = dot(item, spread, TN)
            r.gates[j, at] = (main * wide).astype(BF)
            r.gates[2 + j, at] = (rest * wide).astype(BF)

    back1 = leave(1)
    for c in sums:
        for copy in c.sib + [c.off_r, c.off_l, c.r0, c.r1, c.l0, c.l1]:
            copy.wait_send()

    def gated(pt, lhs):
        out = []
        for g in range(3):
            value = jnp.zeros((lhs.stop - lhs.start, 256), F32)
            rows = r.bmain[pt, :, :, g * 256 : (g + 1) * 256].reshape(256, 256)
            rest = r.brest[pt].reshape(256, 256)
            mask = iota((lhs.stop - lhs.start, 256), 1) % MAIN // 4 == g
            for j in range(2):
                value = value + dot(r.gates[j, lhs], rows)
                value = value + dot(jnp.where(mask, r.gates[2 + j, lhs], jnp.zeros((), BF)), rest)
            out.append(value)
        return out

    for copy in back0:
        copy.wait()
    primal = gated(0, slice(0, 2 * TOK))
    for g in range(3):
        at = slice(g * 256, (g + 1) * 256)
        r.mixed[:, at] = (r.state[0, :, at].astype(F32) + primal[g][:TOK]).astype(BF)
        r.kept[:, at] = r.state[1, :, at].astype(F32) + primal[g][TOK:]
    for copy in back1:
        copy.wait()
    tangent = gated(1, slice(0, TOK))
    for g in range(3):
        at = slice(g * 256, (g + 1) * 256)
        r.mixed_tan[:, at] = (r.kept[:, at] + tangent[g]).astype(BF)


def shards(
    residual_in, residual_tan, queries, keys, values, query_tan, key_tan, value_tan,
    out_proj, shift_mod, scale_mod, router, up_weight, down_weight, expert_ids,
):
    out = jax.ShapeDtypeStruct((TOK, QUARTER), BF)
    return pl.pallas_call(
        block_kernel,
        out_shape=(out, out),
        in_specs=[pl.BlockSpec(memory_space=pl.ANY)] * 15,
        out_specs=(pl.BlockSpec(memory_space=VMEM),) * 2,
        scratch_shapes=list(SCRATCH.values()),
        compiler_params=pltpu.CompilerParams(
            collective_id=1, has_side_effects=True, vmem_limit_bytes=64 * MIB - 64 * 1024
        ),
        name="block",
    )(
        queries, query_tan, keys, values, key_tan, value_tan, out_proj, residual_in, residual_tan,
        up_weight, down_weight, router.T, shift_mod[None], scale_mod[None], expert_ids.T,
    )


def solution(mesh):
    rows, heads = P("ctx", "exp"), P("exp", None)
    in_specs = (rows,) * 8 + (
        heads, P(), P(), P(), P("ctx", None, "exp"), P("ctx", "exp", None), P("ctx", None),
    )
    return jax.shard_map(shards, mesh=mesh, in_specs=in_specs, out_specs=(rows, rows), check_vma=False)
```
